32 devices in a mesh: pb: 8 (over z, y), pa: 4 (over x, core).
Axes of the slice: x: 2, y: 2, z: 4, core: 2. Of those that a mesh axis runs over, the one named last changes fastest.
Arguments:
- queries: float32 [8192, 4096], P('pb'), may hold values from -2.0898438 to 2.0898438
- passages: float32 [1024, 4096], P('pa', 'pb'), may hold values from -0.15625 to 0.15625
- pairs: int32 [96, 2], P('pb'), may hold values from 0 to 31, as said below
- positives: int32 [8192], P('pb'), may hold values from 0 to 1023, as said below
Outputs:
- losses: float32 [8192], P('pb')
- query_grad: float32 [8192, 4096], P('pb', 'pa')
- passage_grad: float32 [1024, 4096], P('pa', 'pb')
The draws below stay inside these ranges and needn't reach their ends.
Inputs may be any that keep to these rules, and one draw needn't show every extreme that they name: Rows k * 12 to (k + 1) * 12 - 1 list query blocks k * 4 to (k + 1) * 4 - 1 only, in column 0; column 1 holds passage blocks. No pair appears twice and every query block appears in at least one pair; the number of pairs of a query block varies. The passage block of positives[i], positives[i] // 256, is listed with the query block of i.
All inputs are finite; a program needn't handle non-finite values.
Results may differ from the reference program's by a relative error of at most 0.0008.
Values sent between devices are 32-bit elements; how exact they have to be, the bound alone decides.
A program may use at most 192 MiB of HBM per device.

```python
import math
import jax
import jax.numpy as jnp
from jax import lax

D = 4096
BLK = 256
QB_DEV = 4
DOC_TILES_SHARE = 1
QBLOCKS = 32
DOCUMENT_TILES = 4
NQ = 8192
NP = 1024
PAIRS_DEV = 12


def layout(key):
    owners = QBLOCKS // QB_DEV
    groups = DOCUMENT_TILES // DOC_TILES_SHARE
    key_rank, key_noise, key_home, key_offset = jax.random.split(jax.random.fold_in(key, 11), 4)
    sorted_indices = jax.random.permutation(key_rank, groups).astype(jnp.int32)
    reward_table = sorted_indices[jnp.arange(DOCUMENT_TILES, dtype=jnp.int32) // DOC_TILES_SHARE] * 2048
    random_whole = jax.random.randint(key_noise, (owners, QB_DEV, DOCUMENT_TILES), 0, 16384, dtype=jnp.int32)
    home_flat = jax.random.randint(key_home, (QBLOCKS,), 0, DOCUMENT_TILES, dtype=jnp.int32)
    home_flat = home_flat.at[0].set(DOCUMENT_TILES - 1)
    home_flat = home_flat.at[QBLOCKS - 1].set(0)
    local_tiles = home_flat.reshape(owners, QB_DEV)
    tile_pairing = jnp.arange(DOCUMENT_TILES, dtype=jnp.int32)
    similarity_grid = jnp.where(tile_pairing[None, None, :] == local_tiles[:, :, None], 1 << 20, random_whole + reward_table[None, None, :])
    combos = jnp.arange(QB_DEV * DOCUMENT_TILES, dtype=jnp.int32)
    ranked = similarity_grid.reshape(owners, QB_DEV * DOCUMENT_TILES) * 1024 + combos[None, :]
    chosen = lax.top_k(ranked, PAIRS_DEV)[1].astype(jnp.int32)
    query_ids = jnp.arange(owners, dtype=jnp.int32)[:, None] * QB_DEV + chosen // DOCUMENT_TILES
    pair_list = jnp.stack([query_ids, chosen % DOCUMENT_TILES], axis=-1).reshape(owners * PAIRS_DEV, 2).astype(jnp.int32)
    offsets = jax.random.randint(key_offset, (QBLOCKS * BLK,), 0, BLK, dtype=jnp.int32)
    offsets = offsets.at[0].set(BLK - 1)
    offsets = offsets.at[QBLOCKS * BLK - 1].set(0)
    home_of_row = home_flat[jnp.arange(QBLOCKS * BLK, dtype=jnp.int32) // BLK]
    positive_ids = (home_of_row * BLK + offsets).astype(jnp.int32)
    return (pair_list, positive_ids)


def alignment(key):
    deviation = D ** (-0.5)
    key_pick, key_level = jax.random.split(jax.random.fold_in(key, 23), 2)
    selected = jax.random.randint(key_pick, (QBLOCKS * BLK,), 0, 64, dtype=jnp.int32) == 0
    selected = selected.at[0].set(True)
    level = jax.random.randint(key_level, (QBLOCKS * BLK,), 0, 3, dtype=jnp.int32)
    strength = jnp.where(level == 0, 110.0, jnp.where(level == 1, 180.0, 300.0)).astype(jnp.float32) * deviation
    return (selected, strength)


def partner_of(positive_ids):
    return positive_ids + 1 - 2 * (positive_ids % 2)


def draw_pairs(key, part):
    return layout(key)[0]


def draw_positives(key, part):
    return layout(key)[1]


def draw_passages(key, part):
    deviation = D ** (-0.5)
    key_base = jax.random.fold_in(jax.random.fold_in(key, 31), 0)
    base = jax.random.truncated_normal(key_base, -5.0, 5.0, (DOCUMENT_TILES * BLK, D), jnp.float32) * deviation
    return jnp.clip(base, -10.0 * deviation, 10.0 * deviation)


def draw_queries(key, part):
    deviation = D ** (-0.5)
    bound = 6000.0 / D + 40.0 * deviation
    key_base = jax.random.fold_in(jax.random.fold_in(key, 41), 0)
    base = jax.random.truncated_normal(key_base, -5.0, 5.0, (QBLOCKS * BLK, D), jnp.float32) * deviation
    passages_now = draw_passages(key, part)
    positive_ids = layout(key)[1]
    selected, strength = alignment(key)
    first_rows = passages_now[positive_ids]
    second_rows = passages_now[partner_of(positive_ids)]
    aligned_rows = strength[:, None] * first_rows + (strength - 2.0 * deviation)[:, None] * second_rows
    base = jnp.where(selected[:, None], aligned_rows, base)
    return jnp.clip(base, -bound, bound)


def setup_inputs(seed: int = 0) -> dict:
    key_list = jax.random.split(jax.random.key(seed), 5)
    return {
        "queries": draw_queries(jax.random.fold_in(key_list[4], 71), 0),
        "passages": draw_passages(jax.random.fold_in(key_list[4], 71), 0),
        "pairs": draw_pairs(jax.random.fold_in(key_list[4], 71), 0),
        "positives": draw_positives(jax.random.fold_in(key_list[4], 71), 0),
    }


low_value = -1e+30
highest = lax.Precision.HIGHEST

def reference(queries, passages, pairs, positives):
    inv_temp = math.sqrt(D)
    columns = jnp.arange(BLK, dtype=jnp.int32)

    def blocks_for(pair_now):
        query_block = lax.dynamic_slice_in_dim(queries, (pair_now[0] * BLK).astype(jnp.int32), BLK, 0)
        passage_block = lax.dynamic_slice_in_dim(passages, (pair_now[1] * BLK).astype(jnp.int32), BLK, 0)
        wanted = lax.dynamic_slice_in_dim(positives, (pair_now[0] * BLK).astype(jnp.int32), BLK, 0) - pair_now[1] * BLK
        hits = columns[None, :] == wanted[:, None]
        return (query_block, passage_block, hits)

    def forward(running, pair_now):
        row_max, row_sum, pos_score = running
        parts_now = blocks_for(pair_now)
        similarity_grid = inv_temp * lax.dot_general(parts_now[0], parts_now[1], (((1,), (1,)), ((), ())), precision=highest, preferred_element_type=jnp.float32)
        start_row = (pair_now[0] * BLK).astype(jnp.int32)
        previous = lax.dynamic_slice_in_dim(row_max, start_row, BLK, 0)
        new_max = jnp.maximum(previous, lax.optimization_barrier(jnp.max(similarity_grid, axis=1)))
        old_sum = lax.dynamic_slice_in_dim(row_sum, start_row, BLK, 0)
        new_sum = old_sum * jnp.exp(previous - new_max) + lax.optimization_barrier(jnp.sum(jnp.exp(similarity_grid - new_max[:, None]), axis=1))
        old_pos = lax.dynamic_slice_in_dim(pos_score, start_row, BLK, 0)
        new_pos = old_pos + lax.optimization_barrier(jnp.sum(jnp.where(parts_now[2], similarity_grid, jnp.zeros_like(similarity_grid)), axis=1))
        row_max = lax.dynamic_update_slice_in_dim(row_max, new_max, start_row, 0)
        row_sum = lax.dynamic_update_slice_in_dim(row_sum, new_sum, start_row, 0)
        pos_score = lax.dynamic_update_slice_in_dim(pos_score, new_pos, start_row, 0)
        return ((row_max, row_sum, pos_score), similarity_grid)
    initial = (jnp.full((NQ,), low_value, jnp.float32), jnp.zeros((NQ,), jnp.float32), jnp.zeros((NQ,), jnp.float32))
    stats, all_tiles = lax.scan(forward, initial, pairs)
    log_norm = stats[0] + jnp.log(stats[1])
    losses = log_norm - stats[2]

    def backward(running, inputs):
        query_grad, passage_grad = running
        pair_now, similarity_grid = inputs
        parts_now = blocks_for(pair_now)
        start_row = (pair_now[0] * BLK).astype(jnp.int32)
        start_col = (pair_now[1] * BLK).astype(jnp.int32)
        norm_rows = lax.dynamic_slice_in_dim(log_norm, start_row, BLK, 0)
        weights = jnp.exp(similarity_grid - norm_rows[:, None]) - parts_now[2].astype(jnp.float32)
        query_term = inv_temp * jnp.dot(weights, parts_now[1], precision=highest, preferred_element_type=jnp.float32)
        passage_term = inv_temp * lax.dot_general(weights, parts_now[0], (((0,), (0,)), ((), ())), precision=highest, preferred_element_type=jnp.float32)
        old_query = lax.dynamic_slice_in_dim(query_grad, start_row, BLK, 0)
        old_passage = lax.dynamic_slice_in_dim(passage_grad, start_col, BLK, 0)
        query_grad = lax.dynamic_update_slice_in_dim(query_grad, old_query + query_term, start_row, 0)
        passage_grad = lax.dynamic_update_slice_in_dim(passage_grad, old_passage + passage_term, start_col, 0)
        return ((query_grad, passage_grad), None)
    grads_init = (jnp.zeros((NQ, D), jnp.float32), jnp.zeros((NP, D), jnp.float32))
    grads, unused = lax.scan(backward, grads_init, (pairs, all_tiles))
    return (losses, grads[0], grads[1])
```

```python
import functools
import math

import jax
import jax.numpy as jnp
from jax import lax
from jax.experimental import pallas as pl
from jax.experimental.pallas import tpu as pltpu
from jax.sharding import PartitionSpec as P

BLK = 256
TILE = 256
low_value = -1e30
MESH = pl.DeviceIdType.MESH
F32 = jnp.float32
BF16 = jnp.bfloat16


def split(value):
    high = value.astype(BF16)
    return high, (value - high.astype(F32)).astype(BF16)


def dot3(left, right, dims):
    def one(a, b):
        return lax.dot_general(a, b, (dims, ((), ())), preferred_element_type=F32)

    return one(left[0], right[1]) + one(left[1], right[0]) + one(left[0], right[0])


def kernel(
    n_pb,
    n_pa,
    scale,
    q_hbm,
    p_hbm,
    pairs_ref,
    pos_ref,
    losses_ref,
    qgrad_hbm,
    pgrad_ref,
    qstage,
    qhi,
    qlo,
    feats,
    slab,
    scores,
    weights_in,
    stats,
    partial,
    y_up,
    y_down,
    z_up,
    z_down,
    qgrad,
    split_w,
    split_p,
    q_sem,
    own_sem,
    out_sem,
    feat_recv,
    zf_send,
    yf_send,
    slab_send,
    slab_recv,
    stat_send,
    stat_recv,
    w_send,
    w_pass,
    w_recv,
    yr_send,
    y_recv,
    zr_send,
    z_recv,
):
    nx = n_pa // 2
    ny = nx
    nz = n_pb // ny
    ratio = n_pb // n_pa
    rows = q_hbm.shape[0]
    chunk = p_hbm.shape[1]
    group_rows = p_hbm.shape[0]
    q_blocks = rows // BLK
    p_blocks = group_rows // BLK
    pair_count = pairs_ref.shape[0]

    me = lax.axis_index("pb")
    ga = lax.axis_index("pa")
    z = me // ny
    y = me % ny
    x = ga // 2
    core = ga % 2
    sibling = x * 2 + 1 - core

    def inside(value, size):
        return jnp.logical_and(value >= 0, value < size)

    def remote(src, dst, send_sem, recv_sem, **where):
        return pltpu.make_async_remote_copy(
            src_ref=src,
            dst_ref=dst,
            send_sem=send_sem,
            recv_sem=recv_sem,
            device_id=where,
            device_id_type=MESH,
        )

    def arrived(buffer, sem):
        remote(buffer, buffer, own_sem, sem, pa=sibling).wait_recv()

    def q_copy(k):
        start = pl.multiple_of(k * chunk, chunk)
        slot = lax.rem(k, 2)
        return pltpu.make_async_copy(
            q_hbm.at[:, pl.ds(start, chunk)], qstage.at[slot], q_sem.at[slot]
        )

    own_copy = pltpu.make_async_copy(p_hbm, feats.at[me], own_sem)
    own_copy.start()
    q_copy(jnp.int32(0)).start()
    q_copy(jnp.int32(1)).start()

    barrier = pltpu.get_barrier_semaphore()
    greeted = jnp.int32(n_pa - 1)
    for step in (1, -1):
        for valid, target in (
            (inside(z + step, nz), (z + step) * ny + y),
            (inside(y + step, ny), z * ny + y + step),
        ):

            @pl.when(valid)
            def _(target=target):
                pl.semaphore_signal(barrier, inc=1, device_id={"pb": target}, device_id_type=MESH)

            greeted = greeted + valid.astype(jnp.int32)
    for i in range(1, n_pa):
        pl.semaphore_signal(
            barrier, inc=1, device_id={"pa": lax.rem(ga + i, n_pa)}, device_id_type=MESH
        )
    pl.semaphore_wait(barrier, greeted)
    own_copy.wait()

    def z_feature(k, d):
        way = 0 if d > 0 else 1
        return remote(
            feats.at[k], feats.at[k], zf_send.at[way, k], feat_recv.at[k], pb=(z + d) * ny + y
        )

    def y_feature(k, e):
        way = 0 if e > 0 else 1
        return remote(
            feats.at[k], feats.at[k], yf_send.at[way, k], feat_recv.at[k], pb=z * ny + y + e
        )

    def slab_feature(k):
        return remote(
            feats.at[k],
            slab.at[ga, k % ratio],
            slab_send.at[k],
            slab_recv.at[ga, k % ratio],
            pa=k // ratio,
        )

    def when_start(valid, make):
        @pl.when(valid)
        def _():
            make().start()

    def when_sent(valid, make):
        @pl.when(valid)
        def _():
            make().wait_send()

    for d in (1, -1):
        when_start(inside(z + d, nz), lambda d=d: z_feature(me, d))
    for e in (1, -1):
        when_start(inside(y + e, ny), lambda e=e: y_feature(me, e))
    when_start(me // ratio != ga, lambda: slab_feature(me))

    @pl.loop(0, n_pb)
    def _(k):
        q_copy(k).wait()
        slot = lax.rem(k, 2)

        @pl.loop(0, rows // 128)
        def _(t):
            part = pl.ds(pl.multiple_of(t * 128, 128), 128)
            high, low = split(qstage[slot, part, :])
            qhi[k, part, :] = high
            qlo[k, part, :] = low

        @pl.when(k + 2 < n_pb)
        def _():
            q_copy(k + 2).start()

    scores[...] = jnp.zeros_like(scores)

    def add_scores(k):
        high, low = split(feats[k])

        @pl.loop(0, rows // TILE)
        def _(t):
            part = pl.ds(pl.multiple_of(t * TILE, TILE), TILE)
            scores[:, part] += dot3(
                (high, low), (qhi[k, part, :], qlo[k, part, :]), ((1,), (1,))
            )

    add_scores(me)

    def y_round(zz):
        for t in range(1, ny):
            for e in (1, -1):
                yy = y + e * t
                k = zz * ny + yy

                @pl.when(inside(yy, ny))
                def _(k=k, e=e):
                    arrived(feats.at[k], feat_recv.at[k])
                    when_start(inside(y - e, ny), lambda: y_feature(k, -e))
                    when_start(k // ratio != ga, lambda: slab_feature(k))
                    add_scores(k)

    @pl.loop(1, nz + 1)
    def _(s):
        for d in (1, -1):
            zz = z + d * s
            k = zz * ny + y

            @pl.when(inside(zz, nz))
            def _(k=k, d=d):
                arrived(feats.at[k], feat_recv.at[k])
                when_start(inside(z - d, nz), lambda: z_feature(k, -d))
                for e in (1, -1):
                    when_start(inside(y + e, ny), lambda e=e: y_feature(k, e))
                when_start(k // ratio != ga, lambda: slab_feature(k))

        for d in (1, -1):
            zz = z + d * s

            @pl.when(inside(zz, nz))
            def _(zz=zz):
                add_scores(zz * ny + y)

        for d in (1, -1):
            zz = z + d * (s - 1)
            once = inside(zz, nz) if d > 0 else jnp.logical_and(inside(zz, nz), s > 1)

            @pl.when(once)
            def _(zz=zz):
                y_round(zz)

    q_first = me * q_blocks
    lane_block = lax.broadcasted_iota(jnp.int32, (1, rows), 1) // BLK

    def live_lanes(p_block):
        found = jnp.zeros((1, rows), jnp.int32)
        for a in range(q_blocks):
            hits = jnp.int32(0)
            for r in range(pair_count):
                same = jnp.logical_and(
                    pairs_ref[r, 0] == q_first + a, pairs_ref[r, 1] == ga * p_blocks + p_block
                )
                hits = hits + same.astype(jnp.int32)
            found = found + jnp.where(lane_block == a, hits, 0)
        return found > 0

    live = [live_lanes(b) for b in range(p_blocks)]
    row_ids = lax.broadcasted_iota(jnp.int32, (BLK, rows), 0)

    def positive_mask(b):
        return row_ids == pos_ref[...] - (ga * p_blocks + b) * BLK

    tops, totals, hits = [], [], []
    for b in range(p_blocks):
        tile = scores[b * BLK : (b + 1) * BLK, :] * scale
        scores[b * BLK : (b + 1) * BLK, :] = tile
        top = jnp.max(tile, axis=0, keepdims=True)
        total = jnp.sum(jnp.exp(tile - top), axis=0, keepdims=True)
        tops.append(jnp.where(live[b], top, low_value))
        totals.append(jnp.where(live[b], total, 0.0))
        hits.append(jnp.sum(jnp.where(positive_mask(b), tile, 0.0), axis=0, keepdims=True))

    def merge(tops, totals):
        joint = functools.reduce(jnp.maximum, tops)
        return joint, sum(t * jnp.exp(m - joint) for m, t in zip(tops, totals))

    top, total = merge(tops, totals)
    stats[ga, 0:1, :] = top
    stats[ga, 1:2, :] = total
    stats[ga, 2:3, :] = sum(hits)
    stats[ga, 3:8, :] = jnp.zeros((5, rows), F32)

    def stat_copy(i):
        return remote(
            stats.at[ga],
            stats.at[ga],
            stat_send.at[i - 1],
            stat_recv.at[ga],
            pa=lax.rem(ga + i, n_pa),
        )

    for i in range(1, n_pa):
        stat_copy(i).start()
    for i in range(1, n_pa):
        other = lax.rem(ga + i, n_pa)
        arrived(stats.at[other], stat_recv.at[other])
    joint, total = merge(
        [stats[g, 0:1, :] for g in range(n_pa)], [stats[g, 1:2, :] for g in range(n_pa)]
    )
    log_norm = joint + jnp.log(total)
    losses_ref[...] = log_norm - sum(stats[g, 2:3, :] for g in range(n_pa))

    for b in range(p_blocks):
        tile = scores[b * BLK : (b + 1) * BLK, :]
        soft = jnp.where(live[b], jnp.exp(tile - log_norm), 0.0)
        weight = soft - positive_mask(b).astype(F32)
        scores[b * BLK : (b + 1) * BLK, :] = weight
        high, low = split(weight)
        split_w[0, b * BLK : (b + 1) * BLK, :] = high
        split_w[1, b * BLK : (b + 1) * BLK, :] = low

    def w_copy(i):
        target = lax.rem(x + i, nx) * 2 + core if i else sibling
        return remote(scores, weights_in.at[ga], w_send.at[i], w_recv.at[ga], pa=target)

    def w_forward(i):
        g = lax.rem(x + i, nx) * 2 + core
        return remote(weights_in.at[g], weights_in.at[g], w_pass.at[i], w_recv.at[g], pa=sibling)

    for i in range(nx):
        w_copy(i).start()

    def form_partial(k):
        left = (split_w[0], split_w[1])
        for n in range(0, chunk, TILE):
            part = pl.ds(n, TILE)
            partial[k, :, part] = scale * dot3(
                left, (qhi[k, :, part], qlo[k, :, part]), ((1,), (0,))
            )

    def y_slot(zz, yy, e):
        return y_up.at[zz, yy - 1] if e > 0 else y_down.at[zz, yy]

    def y_sem(zz, yy, e):
        return y_recv.at[0 if e > 0 else 1, zz, yy - 1 if e > 0 else yy]

    def y_sum(k, zz, yy, e):
        arrived(y_slot(zz, yy, e), y_sem(zz, yy, e))
        partial[k] += y_slot(zz, yy, e)[...]

    def y_partial(zz, yy, e):
        way = 0 if e > 0 else 1
        k = zz * ny + yy
        return remote(
            partial.at[k],
            y_slot(zz, yy, e),
            yr_send.at[way, k],
            y_sem(zz, yy, e),
            pb=z * ny + y + e,
        )

    def each_z(body):
        @pl.loop(0, nz)
        def _(i):
            s = nz - 1 - i
            for d in (1, -1):
                zz = z + d * s
                valid = inside(zz, nz) if d > 0 else jnp.logical_and(inside(zz, nz), s > 0)

                @pl.when(valid)
                def _(zz=zz):
                    body(zz)

    for t in range(ny - 1, 0, -1):
        for e in (1, -1):
            yy = y + e * t

            @pl.when(inside(yy, ny))
            def _(yy=yy, e=e):
                def send_one(zz):
                    k = zz * ny + yy
                    form_partial(k)

                    @pl.when(inside(y - e, ny))
                    def _():
                        y_sum(k, zz, yy, e)

                    y_partial(zz, yy, e).start()

                each_z(send_one)

    each_z(lambda zz: form_partial(zz * ny + y))

    def z_slot(zz, d):
        return z_up.at[zz - 1] if d > 0 else z_down.at[zz]

    def z_sem(zz, d):
        return z_recv.at[0 if d > 0 else 1, zz - 1 if d > 0 else zz]

    def z_partial(zz, d):
        way = 0 if d > 0 else 1
        return remote(
            partial.at[zz * ny + y],
            z_slot(zz, d),
            zr_send.at[way, zz],
            z_sem(zz, d),
            pb=(z + d) * ny + y,
        )

    def y_gather(zz):
        for e in (1, -1):

            @pl.when(inside(y - e, ny))
            def _(e=e):
                y_sum(zz * ny + y, zz, y, e)

    def z_sum(zz, d):
        arrived(z_slot(zz, d), z_sem(zz, d))
        partial[zz * ny + y] += z_slot(zz, d)[...]

    def z_step(s):
        for d in (1, -1):
            zz = z + d * s

            @pl.when(inside(zz, nz))
            def _(zz=zz, d=d):
                y_gather(zz)

                @pl.when(inside(z - d, nz))
                def _():
                    z_sum(zz, d)

                z_partial(zz, d).start()

    def add_query_grad(w_ref, p_refs, first):
        for j in range(ratio):
            high, low = split(p_refs[j][...])
            split_p[j, 0] = high
            split_p[j, 1] = low

        @pl.loop(0, rows // TILE)
        def _(t):
            part = pl.ds(pl.multiple_of(t * TILE, TILE), TILE)
            left = split(w_ref[:, part].T)
            for j in range(ratio):
                cols = pl.ds(j * chunk, chunk)
                term = scale * dot3(left, (split_p[j, 0], split_p[j, 1]), ((1,), (0,)))
                if first:
                    qgrad[part, cols] = term
                else:
                    qgrad[part, cols] += term

    def group_query_grad(g):
        arrived(weights_in.at[g], w_recv.at[g])
        wait_slab(g)
        add_query_grad(weights_in.at[g], [slab.at[g, j] for j in range(ratio)], False)

    def wait_slab(g):
        for j in range(ratio):
            arrived(slab.at[g, j], slab_recv.at[g, j])

    def same_core_query_grad(i):
        g = lax.rem(x + i, nx) * 2 + core
        wait_slab(g)
        add_query_grad(weights_in.at[g], [slab.at[g, j] for j in range(ratio)], False)

    add_query_grad(scores, [feats.at[ga * ratio + j] for j in range(ratio)], True)
    z_step(nz - 1)
    group_query_grad(sibling)
    for s in range(nz - 2, 0, -1):
        z_step(s)
    for i in range(1, nx):
        g = lax.rem(x + i, nx) * 2 + core
        arrived(weights_in.at[g], w_recv.at[g])
        w_forward(i).start()
    for i in range(1, nx):
        same_core_query_grad(i)
    for i in range(1, nx):
        group_query_grad(lax.rem(x + i, nx) * 2 + 1 - core)
    out_copy = pltpu.make_async_copy(qgrad, qgrad_hbm, out_sem)
    out_copy.start()

    y_gather(z)
    for d in (1, -1):

        @pl.when(inside(z - d, nz))
        def _(d=d):
            z_sum(z, d)

    pgrad_ref[...] = partial[me]

    @pl.loop(0, n_pb)
    def _(k):
        zz = k // ny
        yy = k % ny
        when_sent(k // ratio != ga, lambda: slab_feature(k))
        for d in (1, -1):
            behind = zz <= z if d > 0 else zz >= z
            ahead = zz > z if d > 0 else zz < z
            line = yy == y
            when_sent(
                jnp.logical_and(jnp.logical_and(line, behind), inside(z + d, nz)),
                lambda d=d: z_feature(k, d),
            )
            when_sent(jnp.logical_and(line, ahead), lambda d=d: z_partial(zz, d))
        for e in (1, -1):
            behind = yy <= y if e > 0 else yy >= y
            ahead = yy > y if e > 0 else yy < y
            when_sent(jnp.logical_and(behind, inside(y + e, ny)), lambda e=e: y_feature(k, e))
            when_sent(ahead, lambda e=e: y_partial(zz, yy, e))

    for i in range(1, n_pa):
        stat_copy(i).wait_send()
    for i in range(nx):
        w_copy(i).wait_send()
    for i in range(1, nx):
        w_forward(i).wait_send()
    out_copy.wait()


def body(n_pb, n_pa, queries, passages, pairs, positives):
    rows, width = queries.shape
    group_rows, chunk = passages.shape
    nx = n_pa // 2
    ny = nx
    nz = n_pb // ny
    ratio = n_pb // n_pa
    dma = pltpu.SemaphoreType.DMA
    losses, query_grad, passage_grad = pl.pallas_call(
        functools.partial(kernel, n_pb, n_pa, math.sqrt(width)),
        out_shape=(
            jax.ShapeDtypeStruct((1, rows), F32),
            jax.ShapeDtypeStruct((rows, ratio * chunk), F32),
            jax.ShapeDtypeStruct((group_rows, chunk), F32),
        ),
        in_specs=[
            pl.BlockSpec(memory_space=pl.ANY),
            pl.BlockSpec(memory_space=pl.ANY),
            pl.BlockSpec(memory_space=pltpu.SMEM),
            pl.BlockSpec(memory_space=pltpu.VMEM),
        ],
        out_specs=(
            pl.BlockSpec(memory_space=pltpu.VMEM),
            pl.BlockSpec(memory_space=pl.ANY),
            pl.BlockSpec(memory_space=pltpu.VMEM),
        ),
        scratch_shapes=[
            pltpu.VMEM((2, rows, chunk), F32),
            pltpu.VMEM((n_pb, rows, chunk), BF16),
            pltpu.VMEM((n_pb, rows, chunk), BF16),
            pltpu.VMEM((n_pb, group_rows, chunk), F32),
            pltpu.VMEM((n_pa, ratio, group_rows, chunk), F32),
            pltpu.VMEM((group_rows, rows), F32),
            pltpu.VMEM((n_pa, group_rows, rows), F32),
            pltpu.VMEM((n_pa, 8, rows), F32),
            pltpu.VMEM((n_pb, group_rows, chunk), F32),
            pltpu.VMEM((nz, ny - 1, group_rows, chunk), F32),
            pltpu.VMEM((nz, ny - 1, group_rows, chunk), F32),
            pltpu.VMEM((nz - 1, group_rows, chunk), F32),
            pltpu.VMEM((nz - 1, group_rows, chunk), F32),
            pltpu.VMEM((rows, ratio * chunk), F32),
            pltpu.VMEM((2, group_rows, rows), BF16),
            pltpu.VMEM((ratio, 2, group_rows, chunk), BF16),
            dma((2,)),
            dma,
            dma,
            dma((n_pb,)),
            dma((2, n_pb)),
            dma((2, n_pb)),
            dma((n_pb,)),
            dma((n_pa, ratio)),
            dma((n_pa - 1,)),
            dma((n_pa,)),
            dma((nx,)),
            dma((nx,)),
            dma((n_pa,)),
            dma((2, n_pb)),
            dma((2, nz, ny - 1)),
            dma((2, nz)),
            dma((2, nz - 1)),
        ],
        compiler_params=pltpu.CompilerParams(
            collective_id=0, has_side_effects=True, vmem_limit_bytes=62 * 2**20
        ),
    )(queries, passages, pairs, positives.reshape(1, rows))
    return losses.reshape(-1), query_grad, passage_grad


def solution(mesh):
    in_specs = (P("pb", None), P("pa", "pb"), P("pb", None), P("pb"))
    out_specs = (P("pb"), P("pb", "pa"), P("pa", "pb"))
    return jax.shard_map(
        functools.partial(body, mesh.shape["pb"], mesh.shape["pa"]),
        mesh=mesh,
        in_specs=in_specs,
        out_specs=out_specs,
        check_vma=False,
    )
```

```python
import functools
import math

import jax
import jax.numpy as jnp
from jax import lax
from jax.experimental import pallas as pl
from jax.experimental.pallas import tpu as pltpu
from jax.sharding import PartitionSpec as P

BLK = 256
TILE = 256
low_value = -1e30
MESH = pl.DeviceIdType.MESH
F32 = jnp.float32
BF16 = jnp.bfloat16


def split(value):
    high = value.astype(BF16)
    return high, (value - high.astype(F32)).astype(BF16)


def dot3(left, right, dims):
    def one(a, b):
        return lax.dot_general(a, b, (dims, ((), ())), preferred_element_type=F32)

    return one(left[0], right[1]) + one(left[1], right[0]) + one(left[0], right[0])


def kernel(
    n_pb,
    n_pa,
    scale,
    q_hbm,
    p_hbm,
    pairs_ref,
    pos_ref,
    losses_ref,
    qgrad_hbm,
    pgrad_ref,
    qstage,
    qhi,
    qlo,
    feats,
    slab,
    scores,
    weights_in,
    stats,
    partial,
    y_up,
    y_down,
    near_in,
    z_up,
    z_down,
    qgrad,
    split_w,
    split_p,
    q_sem,
    own_sem,
    out_sem,
    feat_recv,
    zf_send,
    yf_send,
    near_send,
    slab_send,
    slab_recv,
    stat_send,
    stat_recv,
    w_send,
    w_pass,
    w_recv,
    yr_send,
    y_recv,
    near_out,
    near_recv,
    zr_send,
    z_recv,
):
    nx = n_pa // 2
    ny = nx
    nz = n_pb // ny
    ratio = n_pb // n_pa
    rows = q_hbm.shape[0]
    chunk = p_hbm.shape[1]
    group_rows = p_hbm.shape[0]
    half = group_rows // 2
    halves = [pl.ds(h * half, half) for h in range(2)]
    near = ny == 2 and nz >= 4
    q_blocks = rows // BLK
    p_blocks = group_rows // BLK

    me = lax.axis_index("pb")
    ga = lax.axis_index("pa")
    z = me // ny
    y = me % ny
    x = ga // 2
    core = ga % 2
    sibling = x * 2 + 1 - core

    def inside(value, size):
        return jnp.logical_and(value >= 0, value < size)

    def remote(src, dst, send_sem, recv_sem, **where):
        return pltpu.make_async_remote_copy(
            src_ref=src,
            dst_ref=dst,
            send_sem=send_sem,
            recv_sem=recv_sem,
            device_id=where,
            device_id_type=MESH,
        )

    def arrived(buffer, sem):
        remote(buffer, buffer, own_sem, sem, pa=sibling).wait_recv()

    def q_copy(k):
        start = pl.multiple_of(k * chunk, chunk)
        slot = lax.rem(k, 2)
        return pltpu.make_async_copy(
            q_hbm.at[:, pl.ds(start, chunk)], qstage.at[slot], q_sem.at[slot]
        )

    own_copy = pltpu.make_async_copy(p_hbm, feats.at[me], own_sem)
    own_copy.start()
    q_copy(jnp.int32(0)).start()
    q_copy(jnp.int32(1)).start()

    barrier = pltpu.get_barrier_semaphore()
    greeted = jnp.int32(n_pa - 1)
    for step in (1, -1):
        for valid, target in (
            (inside(z + step, nz), (z + step) * ny + y),
            (inside(y + step, ny), z * ny + y + step),
        ):

            @pl.when(valid)
            def _(target=target):
                pl.semaphore_signal(barrier, inc=1, device_id={"pb": target}, device_id_type=MESH)

            greeted = greeted + valid.astype(jnp.int32)
    for i in range(1, n_pa):
        pl.semaphore_signal(
            barrier, inc=1, device_id={"pa": lax.rem(ga + i, n_pa)}, device_id_type=MESH
        )
    pl.semaphore_wait(barrier, greeted)
    own_copy.wait()

    def feature(k, h, send_sem, **where):
        ref = feats.at[k, halves[h]]
        return remote(ref, ref, send_sem, feat_recv.at[k, h], **where)

    def z_feature(k, h, d):
        way = 0 if d > 0 else 1
        return feature(k, h, zf_send.at[way, k, h], pb=(z + d) * ny + y)

    def y_feature(k, h, e):
        way = 0 if e > 0 else 1
        return feature(k, h, yf_send.at[way, k, h], pb=z * ny + y + e)

    def near_feature(d):
        way = 0 if d > 0 else 1
        return feature(z * ny + 1 - y, 1, near_send.at[way], pb=(z + d) * ny + y)

    def feature_arrived(k, h):
        arrived(feats.at[k, halves[h]], feat_recv.at[k, h])

    def slab_feature(k):
        return remote(
            feats.at[k],
            slab.at[ga, k % ratio],
            slab_send.at[k],
            slab_recv.at[ga, k % ratio],
            pa=k // ratio,
        )

    def when_start(valid, make):
        @pl.when(valid)
        def _():
            make().start()

    def when_sent(valid, make):
        @pl.when(valid)
        def _():
            make().wait_send()

    for h in range(2):
        for d in (1, -1):
            when_start(inside(z + d, nz), lambda d=d: z_feature(me, h, d))
        for e in (1, -1):
            when_start(inside(y + e, ny), lambda e=e: y_feature(me, h, e))
    when_start(me // ratio != ga, lambda: slab_feature(me))

    @pl.loop(0, n_pb)
    def _(k):
        q_copy(k).wait()
        slot = lax.rem(k, 2)

        @pl.loop(0, rows // 128)
        def _(t):
            part = pl.ds(pl.multiple_of(t * 128, 128), 128)
            high, low = split(qstage[slot, part, :])
            qhi[k, part, :] = high
            qlo[k, part, :] = low

        @pl.when(k + 2 < n_pb)
        def _():
            q_copy(k + 2).start()

    scores[...] = jnp.zeros_like(scores)

    def add_scores(k):
        high, low = split(feats[k])

        @pl.loop(0, rows // TILE)
        def _(t):
            part = pl.ds(pl.multiple_of(t * TILE, TILE), TILE)
            scores[:, part] += dot3(
                (high, low), (qhi[k, part, :], qlo[k, part, :]), ((1,), (1,))
            )

    add_scores(me)

    def y_round(r):
        for d in (1, -1):
            zz = z + d * r
            once = inside(zz, nz) if d > 0 else jnp.logical_and(inside(zz, nz), r > 0)
            for t in range(1, ny):
                for e in (1, -1):
                    yy = y + e * t
                    k = zz * ny + yy

                    @pl.when(jnp.logical_and(once, inside(yy, ny)))
                    def _(k=k, e=e):
                        for h in range(2):
                            feature_arrived(k, h)
                            when_start(inside(y - e, ny), lambda: y_feature(k, h, -e))
                        when_start(k // ratio != ga, lambda: slab_feature(k))
                        add_scores(k)

    @pl.loop(1, nz)
    def _(s):
        for h in range(2):
            for d in (1, -1):
                zz = z + d * s
                k = zz * ny + y

                @pl.when(inside(zz, nz))
                def _(k=k, d=d, h=h):
                    feature_arrived(k, h)
                    when_start(inside(z - d, nz), lambda: z_feature(k, h, -d))
                    for e in (1, -1):
                        whole = s > 1 if near and h == 1 else True
                        when_start(
                            jnp.logical_and(whole, inside(y + e, ny)),
                            lambda e=e: y_feature(k, h, e),
                        )
                    if h == 1:
                        when_start(k // ratio != ga, lambda: slab_feature(k))

        if near:
            for d in (1, -1):
                when_start(
                    jnp.logical_and(s == nz - 2, inside(z + d, nz)), lambda d=d: near_feature(d)
                )

        for d in (1, -1):
            zz = z + d * s

            @pl.when(inside(zz, nz))
            def _(zz=zz):
                add_scores(zz * ny + y)

        @pl.when(s == 1)
        def _():
            y_round(jnp.int32(0))

    @pl.loop(0, nz - 1)
    def _(i):
        y_round(jnp.where(i < nz - 2, i + 2, 1))

    q_first = me * q_blocks
    lane_block = lax.broadcasted_iota(jnp.int32, (1, rows), 1) // BLK

    def live_lanes(p_block):
        same = jnp.logical_and(
            pairs_ref[:, 0:1] - q_first == lane_block,
            pairs_ref[:, 1:2] == ga * p_blocks + p_block,
        )
        return jnp.max(same.astype(jnp.int32), axis=0, keepdims=True) > 0

    live = [live_lanes(b) for b in range(p_blocks)]
    row_ids = lax.broadcasted_iota(jnp.int32, (BLK, rows), 0)

    def positive_mask(b):
        return row_ids == pos_ref[...] - (ga * p_blocks + b) * BLK

    tops, totals, hits = [], [], []
    for b in range(p_blocks):
        tile = scores[b * BLK : (b + 1) * BLK, :] * scale
        scores[b * BLK : (b + 1) * BLK, :] = tile
        top = jnp.max(tile, axis=0, keepdims=True)
        total = jnp.sum(jnp.exp(tile - top), axis=0, keepdims=True)
        tops.append(jnp.where(live[b], top, low_value))
        totals.append(jnp.where(live[b], total, 0.0))
        hits.append(jnp.sum(jnp.where(positive_mask(b), tile, 0.0), axis=0, keepdims=True))

    def merge(tops, totals):
        joint = functools.reduce(jnp.maximum, tops)
        return joint, sum(t * jnp.exp(m - joint) for m, t in zip(tops, totals))

    top, total = merge(tops, totals)
    stats[ga, 0:1, :] = top
    stats[ga, 1:2, :] = total
    stats[ga, 2:3, :] = sum(hits)
    stats[ga, 3:8, :] = jnp.zeros((5, rows), F32)

    def stat_copy(i):
        return remote(
            stats.at[ga],
            stats.at[ga],
            stat_send.at[i - 1],
            stat_recv.at[ga],
            pa=lax.rem(ga + i, n_pa),
        )

    for i in range(1, n_pa):
        stat_copy(i).start()
    for i in range(1, n_pa):
        other = lax.rem(ga + i, n_pa)
        arrived(stats.at[other], stat_recv.at[other])
    joint, total = merge(
        [stats[g, 0:1, :] for g in range(n_pa)], [stats[g, 1:2, :] for g in range(n_pa)]
    )
    log_norm = joint + jnp.log(total)
    losses_ref[...] = log_norm - sum(stats[g, 2:3, :] for g in range(n_pa))

    for b in range(p_blocks):
        tile = scores[b * BLK : (b + 1) * BLK, :]
        soft = jnp.where(live[b], jnp.exp(tile - log_norm), 0.0)
        weight = soft - positive_mask(b).astype(F32)
        scores[b * BLK : (b + 1) * BLK, :] = weight
        high, low = split(weight)
        split_w[0, b * BLK : (b + 1) * BLK, :] = high
        split_w[1, b * BLK : (b + 1) * BLK, :] = low

    def w_copy(i):
        target = lax.rem(x + i, nx) * 2 + core if i else sibling
        return remote(scores, weights_in.at[ga], w_send.at[i], w_recv.at[ga], pa=target)

    def w_forward(i):
        g = lax.rem(x + i, nx) * 2 + core
        return remote(weights_in.at[g], weights_in.at[g], w_pass.at[i], w_recv.at[g], pa=sibling)

    for i in range(nx):
        w_copy(i).start()

    def form_partial(k):
        left = (split_w[0], split_w[1])
        for n in range(0, chunk, TILE):
            part = pl.ds(n, TILE)
            partial[k, :, part] = scale * dot3(
                left, (qhi[k, :, part], qlo[k, :, part]), ((1,), (0,))
            )

    def y_slot(zz, yy, e, h):
        return y_up.at[zz, yy - 1, halves[h]] if e > 0 else y_down.at[zz, yy, halves[h]]

    def y_sem(zz, yy, e, h):
        return y_recv.at[0 if e > 0 else 1, zz, yy - 1 if e > 0 else yy, h]

    def add_partial(k, h, slot, sem):
        arrived(slot, sem)
        partial[k, halves[h]] += slot[...]

    def y_sum(zz, yy, e, h):
        add_partial(zz * ny + yy, h, y_slot(zz, yy, e, h), y_sem(zz, yy, e, h))

    def y_partial(zz, yy, e, h):
        way = 0 if e > 0 else 1
        k = zz * ny + yy
        return remote(
            partial.at[k, halves[h]],
            y_slot(zz, yy, e, h),
            yr_send.at[way, k, h],
            y_sem(zz, yy, e, h),
            pb=z * ny + y + e,
        )

    def near_partial(d):
        way = 0 if d > 0 else 1
        return remote(
            partial.at[(z + d) * ny + 1 - y, halves[1]],
            near_in.at[way],
            near_out.at[way],
            near_recv.at[way],
            pb=(z + d) * ny + y,
        )

    def each_z(body, last):
        @pl.loop(0, nz - last)
        def _(i):
            s = nz - 1 - i
            for d in (1, -1):
                zz = z + d * s
                valid = inside(zz, nz) if d > 0 else jnp.logical_and(inside(zz, nz), s > 0)

                @pl.when(valid)
                def _(zz=zz, d=d):
                    body(zz, d, s)

    for t in range(ny - 1, 0, -1):
        for e in (1, -1):
            yy = y + e * t

            @pl.when(inside(yy, ny))
            def _(yy=yy, e=e):
                def send_one(zz, d, s):
                    form_partial(zz * ny + yy)
                    for h in range(2):

                        @pl.when(inside(y - e, ny))
                        def _(h=h):
                            y_sum(zz, yy, e, h)

                        direct = s > 1 if near and h == 1 else True
                        when_start(direct, lambda: y_partial(zz, yy, e, h))
                    if near:
                        when_start(s == 1, lambda: near_partial(d))

                each_z(send_one, 0)

    each_z(lambda zz, d, s: form_partial(zz * ny + y), 0)

    if near:
        across = z * ny + 1 - y
        for d in (1, -1):
            way = 0 if d > 0 else 1

            @pl.when(inside(z - d, nz))
            def _(way=way):
                add_partial(across, 1, near_in.at[way], near_recv.at[way])

        for e in (1, -1):
            when_start(inside(y + e, ny), lambda e=e: y_partial(z, y + e, e, 1))

    def z_slot(zz, d, h):
        return z_up.at[zz - 1, halves[h]] if d > 0 else z_down.at[zz, halves[h]]

    def z_sem(zz, d, h):
        return z_recv.at[0 if d > 0 else 1, zz - 1 if d > 0 else zz, h]

    def z_partial(zz, d, h):
        way = 0 if d > 0 else 1
        return remote(
            partial.at[zz * ny + y, halves[h]],
            z_slot(zz, d, h),
            zr_send.at[way, zz, h],
            z_sem(zz, d, h),
            pb=(z + d) * ny + y,
        )

    def y_gather(zz, h):
        for e in (1, -1):

            @pl.when(inside(y - e, ny))
            def _(e=e):
                y_sum(zz, y, e, h)

    def z_sum(zz, d, h):
        add_partial(zz * ny + y, h, z_slot(zz, d, h), z_sem(zz, d, h))

    def z_step(s):
        for h in range(2):
            for d in (1, -1):
                zz = z + d * s

                @pl.when(inside(zz, nz))
                def _(zz=zz, d=d, h=h):
                    if not (near and s == 1 and h == 1):
                        y_gather(zz, h)

                    @pl.when(inside(z - d, nz))
                    def _():
                        z_sum(zz, d, h)

                    z_partial(zz, d, h).start()

    def add_query_grad(w_ref, p_refs, first):
        for j in range(ratio):
            high, low = split(p_refs[j][...])
            split_p[j, 0] = high
            split_p[j, 1] = low

        @pl.loop(0, rows // TILE)
        def _(t):
            part = pl.ds(pl.multiple_of(t * TILE, TILE), TILE)
            left = split(w_ref[:, part].T)
            for j in range(ratio):
                cols = pl.ds(j * chunk, chunk)
                term = scale * dot3(left, (split_p[j, 0], split_p[j, 1]), ((1,), (0,)))
                if first:
                    qgrad[part, cols] = term
                else:
                    qgrad[part, cols] += term

    def group_query_grad(g):
        arrived(weights_in.at[g], w_recv.at[g])
        wait_slab(g)
        add_query_grad(weights_in.at[g], [slab.at[g, j] for j in range(ratio)], False)

    def wait_slab(g):
        for j in range(ratio):
            arrived(slab.at[g, j], slab_recv.at[g, j])

    def same_core_query_grad(i):
        g = lax.rem(x + i, nx) * 2 + core
        wait_slab(g)
        add_query_grad(weights_in.at[g], [slab.at[g, j] for j in range(ratio)], False)

    add_query_grad(scores, [feats.at[ga * ratio + j] for j in range(ratio)], True)
    z_step(nz - 1)
    group_query_grad(sibling)
    for s in range(nz - 2, 0, -1):
        z_step(s)
    for i in range(1, nx):
        g = lax.rem(x + i, nx) * 2 + core
        arrived(weights_in.at[g], w_recv.at[g])
        w_forward(i).start()
    for i in range(1, nx):
        same_core_query_grad(i)
    for i in range(1, nx):
        group_query_grad(lax.rem(x + i, nx) * 2 + 1 - core)
    out_copy = pltpu.make_async_copy(qgrad, qgrad_hbm, out_sem)
    out_copy.start()

    for h in range(2):
        for d in (1, -1):

            @pl.when(inside(z - d, nz))
            def _(d=d, h=h):
                z_sum(z, d, h)

        y_gather(z, h)

    pgrad_ref[...] = partial[me]

    @pl.loop(0, n_pb)
    def _(k):
        zz = k // ny
        yy = k % ny
        when_sent(k // ratio != ga, lambda: slab_feature(k))
        for h in range(2):
            far = jnp.abs(zz - z) != 1 if near and h == 1 else True
            for d in (1, -1):
                behind = zz <= z if d > 0 else zz >= z
                ahead = zz > z if d > 0 else zz < z
                line = yy == y
                when_sent(
                    jnp.logical_and(jnp.logical_and(line, behind), inside(z + d, nz)),
                    lambda d=d: z_feature(k, h, d),
                )
                when_sent(jnp.logical_and(line, ahead), lambda d=d: z_partial(zz, d, h))
            for e in (1, -1):
                behind = yy <= y if e > 0 else yy >= y
                ahead = yy > y if e > 0 else yy < y
                when_sent(
                    jnp.logical_and(far, jnp.logical_and(behind, inside(y + e, ny))),
                    lambda e=e: y_feature(k, h, e),
                )
                when_sent(jnp.logical_and(far, ahead), lambda e=e: y_partial(zz, yy, e, h))

    if near:
        for d in (1, -1):
            when_sent(inside(z + d, nz), lambda d=d: near_feature(d))
            when_sent(inside(z + d, nz), lambda d=d: near_partial(d))
    for i in range(1, n_pa):
        stat_copy(i).wait_send()
    for i in range(nx):
        w_copy(i).wait_send()
    for i in range(1, nx):
        w_forward(i).wait_send()
    out_copy.wait()


def body(n_pb, n_pa, queries, passages, pairs, positives):
    rows, width = queries.shape
    group_rows, chunk = passages.shape
    nx = n_pa // 2
    ny = nx
    nz = n_pb // ny
    ratio = n_pb // n_pa
    dma = pltpu.SemaphoreType.DMA
    losses, query_grad, passage_grad = pl.pallas_call(
        functools.partial(kernel, n_pb, n_pa, math.sqrt(width)),
        out_shape=(
            jax.ShapeDtypeStruct((1, rows), F32),
            jax.ShapeDtypeStruct((rows, ratio * chunk), F32),
            jax.ShapeDtypeStruct((group_rows, chunk), F32),
        ),
        in_specs=[
            pl.BlockSpec(memory_space=pl.ANY),
            pl.BlockSpec(memory_space=pl.ANY),
            pl.BlockSpec(memory_space=pltpu.VMEM),
            pl.BlockSpec(memory_space=pltpu.VMEM),
        ],
        out_specs=(
            pl.BlockSpec(memory_space=pltpu.VMEM),
            pl.BlockSpec(memory_space=pl.ANY),
            pl.BlockSpec(memory_space=pltpu.VMEM),
        ),
        scratch_shapes=[
            pltpu.VMEM((2, rows, chunk), F32),
            pltpu.VMEM((n_pb, rows, chunk), BF16),
            pltpu.VMEM((n_pb, rows, chunk), BF16),
            pltpu.VMEM((n_pb, group_rows, chunk), F32),
            pltpu.VMEM((n_pa, ratio, group_rows, chunk), F32),
            pltpu.VMEM((group_rows, rows), F32),
            pltpu.VMEM((n_pa, group_rows, rows), F32),
            pltpu.VMEM((n_pa, 8, rows), F32),
            pltpu.VMEM((n_pb, group_rows, chunk), F32),
            pltpu.VMEM((nz, ny - 1, group_rows, chunk), F32),
            pltpu.VMEM((nz, ny - 1, group_rows, chunk), F32),
            pltpu.VMEM((2, group_rows // 2, chunk), F32),
            pltpu.VMEM((nz - 1, group_rows, chunk), F32),
            pltpu.VMEM((nz - 1, group_rows, chunk), F32),
            pltpu.VMEM((rows, ratio * chunk), F32),
            pltpu.VMEM((2, group_rows, rows), BF16),
            pltpu.VMEM((ratio, 2, group_rows, chunk), BF16),
            dma((2,)),
            dma,
            dma,
            dma((n_pb, 2)),
            dma((2, n_pb, 2)),
            dma((2, n_pb, 2)),
            dma((2,)),
            dma((n_pb,)),
            dma((n_pa, ratio)),
            dma((n_pa - 1,)),
            dma((n_pa,)),
            dma((nx,)),
            dma((nx,)),
            dma((n_pa,)),
            dma((2, n_pb, 2)),
            dma((2, nz, ny - 1, 2)),
            dma((2,)),
            dma((2,)),
            dma((2, nz, 2)),
            dma((2, nz - 1, 2)),
        ],
        compiler_params=pltpu.CompilerParams(
            collective_id=0, has_side_effects=True, vmem_limit_bytes=62 * 2**20
        ),
    )(queries, passages, pairs, positives.reshape(1, rows))
    return losses.reshape(-1), query_grad, passage_grad


def solution(mesh):
    in_specs = (P("pb", None), P("pa", "pb"), P("pb", None), P("pb"))
    out_specs = (P("pb"), P("pb", "pa"), P("pa", "pb"))
    return jax.shard_map(
        functools.partial(body, mesh.shape["pb"], mesh.shape["pa"]),
        mesh=mesh,
        in_specs=in_specs,
        out_specs=out_specs,
        check_vma=False,
    )
```

```python
import functools
import math

import jax
import jax.numpy as jnp
from jax import lax
from jax.experimental import pallas as pl
from jax.experimental.pallas import tpu as pltpu
from jax.sharding import PartitionSpec as P

BLK = 256
TILE = 256
low_value = -1e30
MESH = pl.DeviceIdType.MESH
F32 = jnp.float32
BF16 = jnp.bfloat16


def split(value):
    high = value.astype(BF16)
    return high, (value - high.astype(F32)).astype(BF16)


def dot3(left, right, dims):
    def one(a, b):
        return lax.dot_general(a, b, (dims, ((), ())), preferred_element_type=F32)

    return one(left[0], right[1]) + one(left[1], right[0]) + one(left[0], right[0])


def kernel(
    n_pb,
    n_pa,
    scale,
    q_hbm,
    p_hbm,
    pairs_ref,
    pos_ref,
    losses_ref,
    qgrad_hbm,
    pgrad_ref,
    qstage,
    qhi,
    qlo,
    feats,
    slab,
    scores,
    weights_in,
    stats,
    partial,
    y_up,
    y_down,
    near_in,
    z_up,
    z_down,
    qgrad,
    split_w,
    split_p,
    q_sem,
    own_sem,
    out_sem,
    feat_recv,
    zf_send,
    yf_send,
    near_send,
    slab_send,
    slab_recv,
    stat_send,
    stat_recv,
    w_send,
    w_pass,
    w_recv,
    yr_send,
    y_recv,
    near_out,
    near_recv,
    zr_send,
    z_recv,
):
    nx = n_pa // 2
    ny = nx
    nz = n_pb // ny
    ratio = n_pb // n_pa
    rows = q_hbm.shape[0]
    chunk = p_hbm.shape[1]
    group_rows = p_hbm.shape[0]
    half = group_rows // 2
    halves = [pl.ds(h * half, half) for h in range(2)]
    near = ny == 2 and nz >= 4
    q_blocks = rows // BLK
    p_blocks = group_rows // BLK

    me = lax.axis_index("pb")
    ga = lax.axis_index("pa")
    z = me // ny
    y = me % ny
    x = ga // 2
    core = ga % 2
    sibling = x * 2 + 1 - core

    def inside(value, size):
        return jnp.logical_and(value >= 0, value < size)

    def remote(src, dst, send_sem, recv_sem, **where):
        return pltpu.make_async_remote_copy(
            src_ref=src,
            dst_ref=dst,
            send_sem=send_sem,
            recv_sem=recv_sem,
            device_id=where,
            device_id_type=MESH,
        )

    def arrived(buffer, sem):
        remote(buffer, buffer, own_sem, sem, pa=sibling).wait_recv()

    def q_copy(k):
        start = pl.multiple_of(k * chunk, chunk)
        slot = lax.rem(k, 2)
        return pltpu.make_async_copy(
            q_hbm.at[:, pl.ds(start, chunk)], qstage.at[slot], q_sem.at[slot]
        )

    own_copy = pltpu.make_async_copy(p_hbm, feats.at[me], own_sem)
    own_copy.start()
    q_copy(jnp.int32(0)).start()
    q_copy(jnp.int32(1)).start()

    barrier = pltpu.get_barrier_semaphore()
    greeted = jnp.int32(n_pa - 1)
    for step in (1, -1):
        for valid, target in (
            (inside(z + step, nz), (z + step) * ny + y),
            (inside(y + step, ny), z * ny + y + step),
        ):

            @pl.when(valid)
            def _(target=target):
                pl.semaphore_signal(barrier, inc=1, device_id={"pb": target}, device_id_type=MESH)

            greeted = greeted + valid.astype(jnp.int32)
    for i in range(1, n_pa):
        pl.semaphore_signal(
            barrier, inc=1, device_id={"pa": lax.rem(ga + i, n_pa)}, device_id_type=MESH
        )
    pl.semaphore_wait(barrier, greeted)
    own_copy.wait()

    def feature(k, h, send_sem, **where):
        ref = feats.at[k, halves[h]]
        return remote(ref, ref, send_sem, feat_recv.at[k, h], **where)

    def z_feature(k, h, d):
        way = 0 if d > 0 else 1
        return feature(k, h, zf_send.at[way, k, h], pb=(z + d) * ny + y)

    def y_feature(k, h, e):
        way = 0 if e > 0 else 1
        return feature(k, h, yf_send.at[way, k, h], pb=z * ny + y + e)

    def near_feature(d):
        way = 0 if d > 0 else 1
        return feature(z * ny + 1 - y, 1, near_send.at[way], pb=(z + d) * ny + y)

    def feature_arrived(k, h):
        arrived(feats.at[k, halves[h]], feat_recv.at[k, h])

    def slab_feature(k):
        return remote(
            feats.at[k],
            slab.at[ga, k % ratio],
            slab_send.at[k],
            slab_recv.at[ga, k % ratio],
            pa=k // ratio,
        )

    def when_start(valid, make):
        @pl.when(valid)
        def _():
            make().start()

    def when_sent(valid, make):
        @pl.when(valid)
        def _():
            make().wait_send()

    def send_own(h):
        for d in (1, -1):
            when_start(inside(z + d, nz), lambda d=d: z_feature(me, h, d))
        for e in (1, -1):
            when_start(inside(y + e, ny), lambda e=e: y_feature(me, h, e))

    send_own(0)
    when_start(me // ratio != ga, lambda: slab_feature(me))

    @pl.loop(0, n_pb)
    def _(k):
        q_copy(k).wait()
        slot = lax.rem(k, 2)

        @pl.loop(0, rows // 128)
        def _(t):
            part = pl.ds(pl.multiple_of(t * 128, 128), 128)
            high, low = split(qstage[slot, part, :])
            qhi[k, part, :] = high
            qlo[k, part, :] = low

        @pl.when(k + 2 < n_pb)
        def _():
            q_copy(k + 2).start()

        @pl.when(k == n_pb // 2)
        def _():
            send_own(1)

    scores[...] = jnp.zeros_like(scores)

    def add_scores(k):
        high, low = split(feats[k])

        @pl.loop(0, rows // TILE)
        def _(t):
            part = pl.ds(pl.multiple_of(t * TILE, TILE), TILE)
            scores[:, part] += dot3(
                (high, low), (qhi[k, part, :], qlo[k, part, :]), ((1,), (1,))
            )

    add_scores(me)

    def y_round(r):
        for d in (1, -1):
            zz = z + d * r
            once = inside(zz, nz) if d > 0 else jnp.logical_and(inside(zz, nz), r > 0)
            for t in range(1, ny):
                for e in (1, -1):
                    yy = y + e * t
                    k = zz * ny + yy

                    @pl.when(jnp.logical_and(once, inside(yy, ny)))
                    def _(k=k, e=e):
                        for h in range(2):
                            feature_arrived(k, h)
                            when_start(inside(y - e, ny), lambda: y_feature(k, h, -e))
                        when_start(k // ratio != ga, lambda: slab_feature(k))
                        add_scores(k)

    @pl.loop(1, nz)
    def _(s):
        for h in range(2):
            for d in (1, -1):
                zz = z + d * s
                k = zz * ny + y

                @pl.when(inside(zz, nz))
                def _(k=k, d=d, h=h):
                    feature_arrived(k, h)
                    when_start(inside(z - d, nz), lambda: z_feature(k, h, -d))
                    for e in (1, -1):
                        whole = s > 1 if near and h == 1 else True
                        when_start(
                            jnp.logical_and(whole, inside(y + e, ny)),
                            lambda e=e: y_feature(k, h, e),
                        )
                    if h == 1:
                        when_start(k // ratio != ga, lambda: slab_feature(k))

        if near:
            for d in (1, -1):
                when_start(
                    jnp.logical_and(s == nz - 2, inside(z + d, nz)), lambda d=d: near_feature(d)
                )

        for d in (1, -1):
            zz = z + d * s

            @pl.when(inside(zz, nz))
            def _(zz=zz):
                add_scores(zz * ny + y)

        @pl.when(s == 1)
        def _():
            y_round(jnp.int32(0))

    @pl.loop(0, nz - 1)
    def _(i):
        y_round(jnp.where(i < nz - 2, i + 2, 1))

    q_first = me * q_blocks
    lane_block = lax.broadcasted_iota(jnp.int32, (1, rows), 1) // BLK

    def live_lanes(p_block):
        same = jnp.logical_and(
            pairs_ref[:, 0:1] - q_first == lane_block,
            pairs_ref[:, 1:2] == ga * p_blocks + p_block,
        )
        return jnp.max(same.astype(jnp.int32), axis=0, keepdims=True) > 0

    live = [live_lanes(b) for b in range(p_blocks)]
    row_ids = lax.broadcasted_iota(jnp.int32, (BLK, rows), 0)

    def positive_mask(b):
        return row_ids == pos_ref[...] - (ga * p_blocks + b) * BLK

    tops, totals, hits = [], [], []
    for b in range(p_blocks):
        tile = scores[b * BLK : (b + 1) * BLK, :] * scale
        scores[b * BLK : (b + 1) * BLK, :] = tile
        top = jnp.max(tile, axis=0, keepdims=True)
        total = jnp.sum(jnp.exp(tile - top), axis=0, keepdims=True)
        tops.append(jnp.where(live[b], top, low_value))
        totals.append(jnp.where(live[b], total, 0.0))
        hits.append(jnp.sum(jnp.where(positive_mask(b), tile, 0.0), axis=0, keepdims=True))

    def merge(tops, totals):
        joint = functools.reduce(jnp.maximum, tops)
        return joint, sum(t * jnp.exp(m - joint) for m, t in zip(tops, totals))

    top, total = merge(tops, totals)
    stats[ga, 0:1, :] = top
    stats[ga, 1:2, :] = total
    stats[ga, 2:3, :] = sum(hits)
    stats[ga, 3:8, :] = jnp.zeros((5, rows), F32)

    def stat_copy(i):
        return remote(
            stats.at[ga],
            stats.at[ga],
            stat_send.at[i - 1],
            stat_recv.at[ga],
            pa=lax.rem(ga + i, n_pa),
        )

    for i in range(1, n_pa):
        stat_copy(i).start()
    for i in range(1, n_pa):
        other = lax.rem(ga + i, n_pa)
        arrived(stats.at[other], stat_recv.at[other])
    joint, total = merge(
        [stats[g, 0:1, :] for g in range(n_pa)], [stats[g, 1:2, :] for g in range(n_pa)]
    )
    log_norm = joint + jnp.log(total)
    losses_ref[...] = log_norm - sum(stats[g, 2:3, :] for g in range(n_pa))

    for b in range(p_blocks):
        tile = scores[b * BLK : (b + 1) * BLK, :]
        soft = jnp.where(live[b], jnp.exp(tile - log_norm), 0.0)
        weight = soft - positive_mask(b).astype(F32)
        scores[b * BLK : (b + 1) * BLK, :] = weight
        high, low = split(weight)
        split_w[0, b * BLK : (b + 1) * BLK, :] = high
        split_w[1, b * BLK : (b + 1) * BLK, :] = low

    def w_copy(i):
        target = lax.rem(x + i, nx) * 2 + core if i else sibling
        return remote(scores, weights_in.at[ga], w_send.at[i], w_recv.at[ga], pa=target)

    def w_forward(i):
        g = lax.rem(x + i, nx) * 2 + core
        return remote(weights_in.at[g], weights_in.at[g], w_pass.at[i], w_recv.at[g], pa=sibling)

    for i in range(nx):
        w_copy(i).start()

    def form_partial(k):
        left = (split_w[0], split_w[1])
        for n in range(0, chunk, TILE):
            part = pl.ds(n, TILE)
            partial[k, :, part] = scale * dot3(
                left, (qhi[k, :, part], qlo[k, :, part]), ((1,), (0,))
            )

    def y_slot(zz, yy, e, h):
        return y_up.at[zz, yy - 1, halves[h]] if e > 0 else y_down.at[zz, yy, halves[h]]

    def y_sem(zz, yy, e, h):
        return y_recv.at[0 if e > 0 else 1, zz, yy - 1 if e > 0 else yy, h]

    def add_partial(k, h, slot, sem):
        arrived(slot, sem)
        partial[k, halves[h]] += slot[...]

    def y_sum(zz, yy, e, h):
        add_partial(zz * ny + yy, h, y_slot(zz, yy, e, h), y_sem(zz, yy, e, h))

    def y_partial(zz, yy, e, h):
        way = 0 if e > 0 else 1
        k = zz * ny + yy
        return remote(
            partial.at[k, halves[h]],
            y_slot(zz, yy, e, h),
            yr_send.at[way, k, h],
            y_sem(zz, yy, e, h),
            pb=z * ny + y + e,
        )

    def near_partial(d):
        way = 0 if d > 0 else 1
        return remote(
            partial.at[(z + d) * ny + 1 - y, halves[1]],
            near_in.at[way],
            near_out.at[way],
            near_recv.at[way],
            pb=(z + d) * ny + y,
        )

    def each_z(body, last):
        @pl.loop(0, nz - last)
        def _(i):
            s = nz - 1 - i
            for d in (1, -1):
                zz = z + d * s
                valid = inside(zz, nz) if d > 0 else jnp.logical_and(inside(zz, nz), s > 0)

                @pl.when(valid)
                def _(zz=zz, d=d):
                    body(zz, d, s)

    across = 1 - y
    farthest = jnp.maximum(z, nz - 1 - z)

    def across_each(s, act):
        for d in (1, -1) if not (isinstance(s, int) and s == 0) else (1,):
            for e in (1, -1):
                zz = z + d * s

                @pl.when(jnp.logical_and(inside(zz, nz), inside(y + e, ny)))
                def _(zz=zz, e=e):
                    act(zz, e)

    def across_start(s, h):
        across_each(s, lambda zz, e: y_partial(zz, across, e, h).start())

    def across_sent(s, h):
        across_each(s, lambda zz, e: y_partial(zz, across, e, h).wait_send())

    if near:
        def form_across(zz, d, s):
            form_partial(zz * ny + across)
            when_start(s == 1, lambda: near_partial(d))

            @pl.when(s == farthest)
            def _():
                for e in (1, -1):
                    when_start(inside(y + e, ny), lambda e=e: y_partial(zz, across, e, 0))

        each_z(form_across, 0)
        across_start(farthest, 1)
    else:
        for t in range(ny - 1, 0, -1):
            for e in (1, -1):
                yy = y + e * t

                @pl.when(inside(yy, ny))
                def _(yy=yy, e=e):
                    def send_one(zz, d, s):
                        form_partial(zz * ny + yy)
                        for h in range(2):

                            @pl.when(inside(y - e, ny))
                            def _(h=h):
                                y_sum(zz, yy, e, h)

                            y_partial(zz, yy, e, h).start()

                    each_z(send_one, 0)

    each_z(lambda zz, d, s: form_partial(zz * ny + y), 0)

    def across_next(s, h):
        if s > 1 or h == 0:

            @pl.when(farthest >= s)
            def _():
                across_sent(s, h)
                if s > 2 or h == 0:
                    across_start(s - 1, h)

        if s == 1 and h == 1:
            for d in (1, -1):
                way = 0 if d > 0 else 1

                @pl.when(inside(z - d, nz))
                def _(way=way):
                    add_partial(z * ny + across, 1, near_in.at[way], near_recv.at[way])

            across_start(0, 1)

    def z_slot(zz, d, h):
        return z_up.at[zz - 1, halves[h]] if d > 0 else z_down.at[zz, halves[h]]

    def z_sem(zz, d, h):
        return z_recv.at[0 if d > 0 else 1, zz - 1 if d > 0 else zz, h]

    def z_partial(zz, d, h):
        way = 0 if d > 0 else 1
        return remote(
            partial.at[zz * ny + y, halves[h]],
            z_slot(zz, d, h),
            zr_send.at[way, zz, h],
            z_sem(zz, d, h),
            pb=(z + d) * ny + y,
        )

    def y_gather(zz, h):
        for e in (1, -1):

            @pl.when(inside(y - e, ny))
            def _(e=e):
                y_sum(zz, y, e, h)

    def z_sum(zz, d, h):
        add_partial(zz * ny + y, h, z_slot(zz, d, h), z_sem(zz, d, h))

    def z_step(s):
        for h in range(2):
            if near:
                across_next(s, h)
            for d in (1, -1):
                zz = z + d * s

                @pl.when(inside(zz, nz))
                def _(zz=zz, d=d, h=h):
                    if not (near and s == 1 and h == 1):
                        y_gather(zz, h)

                    @pl.when(inside(z - d, nz))
                    def _():
                        z_sum(zz, d, h)

                    z_partial(zz, d, h).start()

    def add_query_grad(w_ref, p_refs, first):
        for j in range(ratio):
            high, low = split(p_refs[j][...])
            split_p[j, 0] = high
            split_p[j, 1] = low

        @pl.loop(0, rows // TILE)
        def _(t):
            part = pl.ds(pl.multiple_of(t * TILE, TILE), TILE)
            left = split(w_ref[:, part].T)
            for j in range(ratio):
                cols = pl.ds(j * chunk, chunk)
                term = scale * dot3(left, (split_p[j, 0], split_p[j, 1]), ((1,), (0,)))
                if first:
                    qgrad[part, cols] = term
                else:
                    qgrad[part, cols] += term

    def group_query_grad(g):
        arrived(weights_in.at[g], w_recv.at[g])
        wait_slab(g)
        add_query_grad(weights_in.at[g], [slab.at[g, j] for j in range(ratio)], False)

    def wait_slab(g):
        for j in range(ratio):
            arrived(slab.at[g, j], slab_recv.at[g, j])

    def same_core_query_grad(i):
        g = lax.rem(x + i, nx) * 2 + core
        wait_slab(g)
        add_query_grad(weights_in.at[g], [slab.at[g, j] for j in range(ratio)], False)

    z_step(nz - 1)
    add_query_grad(scores, [feats.at[ga * ratio + j] for j in range(ratio)], True)
    group_query_grad(sibling)
    for s in range(nz - 2, 0, -1):
        z_step(s)
    for i in range(1, nx):
        g = lax.rem(x + i, nx) * 2 + core
        arrived(weights_in.at[g], w_recv.at[g])
        w_forward(i).start()
    for i in range(1, nx):
        same_core_query_grad(i)
    for i in range(1, nx):
        group_query_grad(lax.rem(x + i, nx) * 2 + 1 - core)
    out_copy = pltpu.make_async_copy(qgrad, qgrad_hbm, out_sem)
    out_copy.start()

    for h in range(2):
        for d in (1, -1):

            @pl.when(inside(z - d, nz))
            def _(d=d, h=h):
                z_sum(z, d, h)

        y_gather(z, h)

    pgrad_ref[...] = partial[me]

    @pl.loop(0, n_pb)
    def _(k):
        zz = k // ny
        yy = k % ny
        when_sent(k // ratio != ga, lambda: slab_feature(k))
        for h in range(2):
            far = jnp.abs(zz - z) != 1 if near and h == 1 else True
            unsent = zz == z if near else True
            for d in (1, -1):
                behind = zz <= z if d > 0 else zz >= z
                ahead = zz > z if d > 0 else zz < z
                line = yy == y
                when_sent(
                    jnp.logical_and(jnp.logical_and(line, behind), inside(z + d, nz)),
                    lambda d=d: z_feature(k, h, d),
                )
                when_sent(jnp.logical_and(line, ahead), lambda d=d: z_partial(zz, d, h))
            for e in (1, -1):
                behind = yy <= y if e > 0 else yy >= y
                ahead = yy > y if e > 0 else yy < y
                when_sent(
                    jnp.logical_and(far, jnp.logical_and(behind, inside(y + e, ny))),
                    lambda e=e: y_feature(k, h, e),
                )
                when_sent(jnp.logical_and(unsent, ahead), lambda e=e: y_partial(zz, yy, e, h))

    if near:
        for d in (1, -1):
            when_sent(inside(z + d, nz), lambda d=d: near_feature(d))
            when_sent(inside(z + d, nz), lambda d=d: near_partial(d))
    for i in range(1, n_pa):
        stat_copy(i).wait_send()
    for i in range(nx):
        w_copy(i).wait_send()
    for i in range(1, nx):
        w_forward(i).wait_send()
    out_copy.wait()


def body(n_pb, n_pa, queries, passages, pairs, positives):
    rows, width = queries.shape
    group_rows, chunk = passages.shape
    nx = n_pa // 2
    ny = nx
    nz = n_pb // ny
    ratio = n_pb // n_pa
    dma = pltpu.SemaphoreType.DMA
    losses, query_grad, passage_grad = pl.pallas_call(
        functools.partial(kernel, n_pb, n_pa, math.sqrt(width)),
        out_shape=(
            jax.ShapeDtypeStruct((1, rows), F32),
            jax.ShapeDtypeStruct((rows, ratio * chunk), F32),
            jax.ShapeDtypeStruct((group_rows, chunk), F32),
        ),
        in_specs=[
            pl.BlockSpec(memory_space=pl.ANY),
            pl.BlockSpec(memory_space=pl.ANY),
            pl.BlockSpec(memory_space=pltpu.VMEM),
            pl.BlockSpec(memory_space=pltpu.VMEM),
        ],
        out_specs=(
            pl.BlockSpec(memory_space=pltpu.VMEM),
            pl.BlockSpec(memory_space=pl.ANY),
            pl.BlockSpec(memory_space=pltpu.VMEM),
        ),
        scratch_shapes=[
            pltpu.VMEM((2, rows, chunk), F32),
            pltpu.VMEM((n_pb, rows, chunk), BF16),
            pltpu.VMEM((n_pb, rows, chunk), BF16),
            pltpu.VMEM((n_pb, group_rows, chunk), F32),
            pltpu.VMEM((n_pa, ratio, group_rows, chunk), F32),
            pltpu.VMEM((group_rows, rows), F32),
            pltpu.VMEM((n_pa, group_rows, rows), F32),
            pltpu.VMEM((n_pa, 8, rows), F32),
            pltpu.VMEM((n_pb, group_rows, chunk), F32),
            pltpu.VMEM((nz, ny - 1, group_rows, chunk), F32),
            pltpu.VMEM((nz, ny - 1, group_rows, chunk), F32),
            pltpu.VMEM((2, group_rows // 2, chunk), F32),
            pltpu.VMEM((nz - 1, group_rows, chunk), F32),
            pltpu.VMEM((nz - 1, group_rows, chunk), F32),
            pltpu.VMEM((rows, ratio * chunk), F32),
            pltpu.VMEM((2, group_rows, rows), BF16),
            pltpu.VMEM((ratio, 2, group_rows, chunk), BF16),
            dma((2,)),
            dma,
            dma,
            dma((n_pb, 2)),
            dma((2, n_pb, 2)),
            dma((2, n_pb, 2)),
            dma((2,)),
            dma((n_pb,)),
            dma((n_pa, ratio)),
            dma((n_pa - 1,)),
            dma((n_pa,)),
            dma((nx,)),
            dma((nx,)),
            dma((n_pa,)),
            dma((2, n_pb, 2)),
            dma((2, nz, ny - 1, 2)),
            dma((2,)),
            dma((2,)),
            dma((2, nz, 2)),
            dma((2, nz - 1, 2)),
        ],
        compiler_params=pltpu.CompilerParams(
            collective_id=0, has_side_effects=True, vmem_limit_bytes=62 * 2**20
        ),
    )(queries, passages, pairs, positives.reshape(1, rows))
    return losses.reshape(-1), query_grad, passage_grad


def solution(mesh):
    in_specs = (P("pb", None), P("pa", "pb"), P("pb", None), P("pb"))
    out_specs = (P("pb"), P("pb", "pa"), P("pa", "pb"))
    return jax.shard_map(
        functools.partial(body, mesh.shape["pb"], mesh.shape["pa"]),
        mesh=mesh,
        in_specs=in_specs,
        out_specs=out_specs,
        check_vma=False,
    )
```

```python
import functools
import math

import jax
import jax.numpy as jnp
from jax import lax
from jax.experimental import pallas as pl
from jax.experimental.pallas import tpu as pltpu
from jax.sharding import PartitionSpec as P

BLK = 256
TILE = 256
low_value = -1e30
MESH = pl.DeviceIdType.MESH
F32 = jnp.float32
BF16 = jnp.bfloat16


def split(value):
    high = value.astype(BF16)
    return high, (value - high.astype(F32)).astype(BF16)


def dot3(left, right, dims):
    def one(a, b):
        return lax.dot_general(a, b, (dims, ((), ())), preferred_element_type=F32)

    return one(left[0], right[1]) + one(left[1], right[0]) + one(left[0], right[0])


def kernel(
    n_pb,
    n_pa,
    scale,
    q_hbm,
    p_hbm,
    pairs_ref,
    pos_ref,
    losses_ref,
    qgrad_hbm,
    pgrad_ref,
    w_out,
    slab_out,
    qstage,
    qhi,
    qlo,
    feats,
    slab,
    scores,
    weights_in,
    stats,
    partial,
    y_up,
    y_down,
    near_in,
    z_up,
    z_down,
    qgrad,
    split_w,
    split_p,
    q_sem,
    own_sem,
    out_sem,
    feat_recv,
    zf_send,
    yf_send,
    near_send,
    slab_send,
    slab_recv,
    stat_send,
    stat_recv,
    w_send,
    w_pass,
    w_recv,
    yr_send,
    y_recv,
    near_out,
    near_recv,
    zr_send,
    z_recv,
):
    nx = n_pa // 2
    ny = nx
    nz = n_pb // ny
    ratio = n_pb // n_pa
    rows = q_hbm.shape[0]
    chunk = p_hbm.shape[1]
    group_rows = p_hbm.shape[0]
    half = group_rows // 2
    halves = [pl.ds(h * half, half) for h in range(2)]
    near = ny == 2 and nz >= 4
    q_blocks = rows // BLK
    p_blocks = group_rows // BLK

    me = lax.axis_index("pb")
    ga = lax.axis_index("pa")
    z = me // ny
    y = me % ny
    x = ga // 2
    core = ga % 2
    sibling = x * 2 + 1 - core

    def inside(value, size):
        return jnp.logical_and(value >= 0, value < size)

    def remote(src, dst, send_sem, recv_sem, **where):
        return pltpu.make_async_remote_copy(
            src_ref=src,
            dst_ref=dst,
            send_sem=send_sem,
            recv_sem=recv_sem,
            device_id=where,
            device_id_type=MESH,
        )

    def arrived(buffer, sem):
        remote(buffer, buffer, own_sem, sem, pa=sibling).wait_recv()

    def q_copy(k):
        start = pl.multiple_of(k * chunk, chunk)
        slot = lax.rem(k, 2)
        return pltpu.make_async_copy(
            q_hbm.at[:, pl.ds(start, chunk)], qstage.at[slot], q_sem.at[slot]
        )

    own_copy = pltpu.make_async_copy(p_hbm, feats.at[me], own_sem)
    own_copy.start()
    q_copy(jnp.int32(0)).start()
    q_copy(jnp.int32(1)).start()

    barrier = pltpu.get_barrier_semaphore()
    greeted = jnp.int32(n_pa - 1)
    for step in (1, -1):
        for valid, target in (
            (inside(z + step, nz), (z + step) * ny + y),
            (inside(y + step, ny), z * ny + y + step),
        ):

            @pl.when(valid)
            def _(target=target):
                pl.semaphore_signal(barrier, inc=1, device_id={"pb": target}, device_id_type=MESH)

            greeted = greeted + valid.astype(jnp.int32)
    for i in range(1, n_pa):
        pl.semaphore_signal(
            barrier, inc=1, device_id={"pa": lax.rem(ga + i, n_pa)}, device_id_type=MESH
        )
    pl.semaphore_wait(barrier, greeted)
    own_copy.wait()

    def feature(k, h, send_sem, **where):
        ref = feats.at[k, halves[h]]
        return remote(ref, ref, send_sem, feat_recv.at[k, h], **where)

    def z_feature(k, h, d):
        way = 0 if d > 0 else 1
        return feature(k, h, zf_send.at[way, k, h], pb=(z + d) * ny + y)

    def y_feature(k, h, e):
        way = 0 if e > 0 else 1
        return feature(k, h, yf_send.at[way, k, h], pb=z * ny + y + e)

    def near_feature(d):
        way = 0 if d > 0 else 1
        return feature(z * ny + 1 - y, 1, near_send.at[way], pb=(z + d) * ny + y)

    def feature_arrived(k, h):
        arrived(feats.at[k, halves[h]], feat_recv.at[k, h])

    def slab_feature(k, h):
        return remote(
            feats.at[k, halves[h]],
            slab.at[ga, k % ratio, halves[h]],
            slab_send.at[k, h],
            slab_recv.at[ga, k % ratio, h],
            pa=k // ratio,
        )

    def when_start(valid, make):
        @pl.when(valid)
        def _():
            make().start()

    def when_sent(valid, make):
        @pl.when(valid)
        def _():
            make().wait_send()

    def send_own(h):
        for d in (1, -1):
            when_start(inside(z + d, nz), lambda d=d: z_feature(me, h, d))
        for e in (1, -1):
            when_start(inside(y + e, ny), lambda e=e: y_feature(me, h, e))

    send_own(0)
    for h in range(2):
        when_start(me // ratio != ga, lambda: slab_feature(me, h))

    @pl.loop(0, n_pb)
    def _(k):
        q_copy(k).wait()
        slot = lax.rem(k, 2)

        @pl.loop(0, rows // 128)
        def _(t):
            part = pl.ds(pl.multiple_of(t * 128, 128), 128)
            high, low = split(qstage[slot, part, :])
            qhi[k, part, :] = high
            qlo[k, part, :] = low

        @pl.when(k + 2 < n_pb)
        def _():
            q_copy(k + 2).start()

        @pl.when(k == n_pb // 2)
        def _():
            send_own(1)

    scores[...] = jnp.zeros_like(scores)

    def add_scores(k):
        high, low = split(feats[k])

        @pl.loop(0, rows // TILE)
        def _(t):
            part = pl.ds(pl.multiple_of(t * TILE, TILE), TILE)
            scores[:, part] += dot3(
                (high, low), (qhi[k, part, :], qlo[k, part, :]), ((1,), (1,))
            )

    add_scores(me)

    def y_round(r, parts, score):
        for d in (1, -1):
            zz = z + d * r
            once = inside(zz, nz) if d > 0 else jnp.logical_and(inside(zz, nz), r > 0)
            for t in range(1, ny):
                for e in (1, -1):
                    yy = y + e * t
                    k = zz * ny + yy

                    @pl.when(jnp.logical_and(once, inside(yy, ny)))
                    def _(k=k, e=e):
                        for h in parts:
                            feature_arrived(k, h)
                            when_start(inside(y - e, ny), lambda: y_feature(k, h, -e))
                            when_start(k // ratio != ga, lambda: slab_feature(k, h))
                        if score:
                            add_scores(k)

    @pl.loop(1, nz)
    def _(s):
        for h in range(2):
            for d in (1, -1):
                zz = z + d * s
                k = zz * ny + y

                @pl.when(inside(zz, nz))
                def _(k=k, d=d, h=h):
                    feature_arrived(k, h)
                    when_start(inside(z - d, nz), lambda: z_feature(k, h, -d))
                    for e in (1, -1):
                        whole = s > 1 if near and h == 1 else True
                        when_start(
                            jnp.logical_and(whole, inside(y + e, ny)),
                            lambda e=e: y_feature(k, h, e),
                        )
                    when_start(k // ratio != ga, lambda: slab_feature(k, h))

        if near:
            for d in (1, -1):
                when_start(
                    jnp.logical_and(s == nz - 2, inside(z + d, nz)), lambda d=d: near_feature(d)
                )

        for d in (1, -1):
            zz = z + d * s

            @pl.when(inside(zz, nz))
            def _(zz=zz):
                add_scores(zz * ny + y)

        @pl.when(s == 1)
        def _():
            y_round(jnp.int32(0), (0, 1), True)

        @pl.when(s > 1)
        def _():
            y_round(s - 1, (0,), False)

    y_round(nz - 1, (0,), False)

    @pl.loop(0, nz - 1)
    def _(i):
        y_round(jnp.where(i < nz - 2, i + 2, 1), (1,), True)

    q_first = me * q_blocks
    lane_block = lax.broadcasted_iota(jnp.int32, (1, rows), 1) // BLK

    def live_lanes(p_block):
        found = jnp.zeros((1, rows), jnp.int32)
        for r in range(pairs_ref.shape[1]):
            same = jnp.logical_and(
                pairs_ref[0:1, r : r + 1] - q_first == lane_block,
                pairs_ref[1:2, r : r + 1] == ga * p_blocks + p_block,
            )
            found = found + same.astype(jnp.int32)
        return found > 0

    live = [live_lanes(b) for b in range(p_blocks)]
    row_ids = lax.broadcasted_iota(jnp.int32, (BLK, rows), 0)

    def positive_mask(b):
        return row_ids == pos_ref[...] - (ga * p_blocks + b) * BLK

    tops, totals, hits = [], [], []
    for b in range(p_blocks):
        tile = scores[b * BLK : (b + 1) * BLK, :] * scale
        scores[b * BLK : (b + 1) * BLK, :] = tile
        top = jnp.max(tile, axis=0, keepdims=True)
        total = jnp.sum(jnp.exp(tile - top), axis=0, keepdims=True)
        tops.append(jnp.where(live[b], top, low_value))
        totals.append(jnp.where(live[b], total, 0.0))
        hits.append(jnp.sum(jnp.where(positive_mask(b), tile, 0.0), axis=0, keepdims=True))

    def merge(tops, totals):
        joint = functools.reduce(jnp.maximum, tops)
        return joint, sum(t * jnp.exp(m - joint) for m, t in zip(tops, totals))

    top, total = merge(tops, totals)
    stats[ga, 0:1, :] = top
    stats[ga, 1:2, :] = total
    stats[ga, 2:3, :] = sum(hits)
    stats[ga, 3:8, :] = jnp.zeros((5, rows), F32)

    def stat_copy(i):
        return remote(
            stats.at[ga],
            stats.at[ga],
            stat_send.at[i - 1],
            stat_recv.at[ga],
            pa=lax.rem(ga + i, n_pa),
        )

    for i in range(1, n_pa):
        stat_copy(i).start()
    for i in range(1, n_pa):
        other = lax.rem(ga + i, n_pa)
        arrived(stats.at[other], stat_recv.at[other])
    joint, total = merge(
        [stats[g, 0:1, :] for g in range(n_pa)], [stats[g, 1:2, :] for g in range(n_pa)]
    )
    log_norm = joint + jnp.log(total)
    losses_ref[...] = log_norm - sum(stats[g, 2:3, :] for g in range(n_pa))

    for b in range(p_blocks):
        tile = scores[b * BLK : (b + 1) * BLK, :]
        soft = jnp.where(live[b], jnp.exp(tile - log_norm), 0.0)
        weight = soft - positive_mask(b).astype(F32)
        scores[b * BLK : (b + 1) * BLK, :] = weight
        high, low = split(weight)
        split_w[0, b * BLK : (b + 1) * BLK, :] = high
        split_w[1, b * BLK : (b + 1) * BLK, :] = low

    def w_copy(i):
        target = lax.rem(x + i, nx) * 2 + core if i else sibling
        return remote(scores, weights_in.at[ga], w_send.at[i], w_recv.at[ga], pa=target)

    def w_forward(i):
        g = lax.rem(x + i, nx) * 2 + core
        return remote(weights_in.at[g], weights_in.at[g], w_pass.at[i], w_recv.at[g], pa=sibling)

    for i in range(nx):
        w_copy(i).start()

    def form_partial(k):
        left = (split_w[0], split_w[1])
        for n in range(0, chunk, TILE):
            part = pl.ds(n, TILE)
            partial[k, :, part] = scale * dot3(
                left, (qhi[k, :, part], qlo[k, :, part]), ((1,), (0,))
            )

    def y_slot(zz, yy, e, h):
        return y_up.at[zz, yy - 1, halves[h]] if e > 0 else y_down.at[zz, yy, halves[h]]

    def y_sem(zz, yy, e, h):
        return y_recv.at[0 if e > 0 else 1, zz, yy - 1 if e > 0 else yy, h]

    def add_partial(k, h, slot, sem):
        arrived(slot, sem)
        partial[k, halves[h]] += slot[...]

    def y_sum(zz, yy, e, h):
        add_partial(zz * ny + yy, h, y_slot(zz, yy, e, h), y_sem(zz, yy, e, h))

    def y_partial(zz, yy, e, h):
        way = 0 if e > 0 else 1
        k = zz * ny + yy
        return remote(
            partial.at[k, halves[h]],
            y_slot(zz, yy, e, h),
            yr_send.at[way, k, h],
            y_sem(zz, yy, e, h),
            pb=z * ny + y + e,
        )

    def near_partial(d):
        way = 0 if d > 0 else 1
        return remote(
            partial.at[(z + d) * ny + 1 - y, halves[1]],
            near_in.at[way],
            near_out.at[way],
            near_recv.at[way],
            pb=(z + d) * ny + y,
        )

    def each_z(body, last):
        @pl.loop(0, nz - last)
        def _(i):
            s = nz - 1 - i
            for d in (1, -1):
                zz = z + d * s
                valid = inside(zz, nz) if d > 0 else jnp.logical_and(inside(zz, nz), s > 0)

                @pl.when(valid)
                def _(zz=zz, d=d):
                    body(zz, d, s)

    across = 1 - y
    farthest = jnp.maximum(z, nz - 1 - z)

    def across_each(s, act):
        for d in (1, -1) if not (isinstance(s, int) and s == 0) else (1,):
            for e in (1, -1):
                zz = z + d * s

                @pl.when(jnp.logical_and(inside(zz, nz), inside(y + e, ny)))
                def _(zz=zz, e=e):
                    act(zz, e)

    def across_start(s, h):
        across_each(s, lambda zz, e: y_partial(zz, across, e, h).start())

    def across_sent(s, h):
        across_each(s, lambda zz, e: y_partial(zz, across, e, h).wait_send())

    if near:
        def form_across(zz, d, s):
            form_partial(zz * ny + across)
            when_start(s == 1, lambda: near_partial(d))

            @pl.when(s == farthest)
            def _():
                for e in (1, -1):
                    when_start(inside(y + e, ny), lambda e=e: y_partial(zz, across, e, 0))

        each_z(form_across, 0)
        across_start(farthest, 1)
    else:
        for t in range(ny - 1, 0, -1):
            for e in (1, -1):
                yy = y + e * t

                @pl.when(inside(yy, ny))
                def _(yy=yy, e=e):
                    def send_one(zz, d, s):
                        form_partial(zz * ny + yy)
                        for h in range(2):

                            @pl.when(inside(y - e, ny))
                            def _(h=h):
                                y_sum(zz, yy, e, h)

                            y_partial(zz, yy, e, h).start()

                    each_z(send_one, 0)

    each_z(lambda zz, d, s: form_partial(zz * ny + y), 0)

    def across_next(s, h):
        if s > 1 or h == 0:

            @pl.when(farthest >= s)
            def _():
                across_sent(s, h)
                if s > 2 or h == 0:
                    across_start(s - 1, h)

        if s == 1 and h == 1:
            for d in (1, -1):
                way = 0 if d > 0 else 1

                @pl.when(inside(z - d, nz))
                def _(way=way):
                    add_partial(z * ny + across, 1, near_in.at[way], near_recv.at[way])

            across_start(0, 1)

    def z_slot(zz, d, h):
        return z_up.at[zz - 1, halves[h]] if d > 0 else z_down.at[zz, halves[h]]

    def z_sem(zz, d, h):
        return z_recv.at[0 if d > 0 else 1, zz - 1 if d > 0 else zz, h]

    def z_partial(zz, d, h):
        way = 0 if d > 0 else 1
        return remote(
            partial.at[zz * ny + y, halves[h]],
            z_slot(zz, d, h),
            zr_send.at[way, zz, h],
            z_sem(zz, d, h),
            pb=(z + d) * ny + y,
        )

    def y_gather(zz, h):
        for e in (1, -1):

            @pl.when(inside(y - e, ny))
            def _(e=e):
                y_sum(zz, y, e, h)

    def z_sum(zz, d, h):
        add_partial(zz * ny + y, h, z_slot(zz, d, h), z_sem(zz, d, h))

    def z_step(s):
        for h in range(2):
            if near:
                across_next(s, h)
            for d in (1, -1):
                zz = z + d * s

                @pl.when(inside(zz, nz))
                def _(zz=zz, d=d, h=h):
                    if not (near and s == 1 and h == 1):
                        y_gather(zz, h)

                    @pl.when(inside(z - d, nz))
                    def _():
                        z_sum(zz, d, h)

                    z_partial(zz, d, h).start()

    def add_query_grad(w_ref, p_refs, first):
        for j in range(ratio):
            high, low = split(p_refs[j][...])
            split_p[j, 0] = high
            split_p[j, 1] = low

        @pl.loop(0, rows // TILE)
        def _(t):
            part = pl.ds(pl.multiple_of(t * TILE, TILE), TILE)
            left = split(w_ref[:, part].T)
            for j in range(ratio):
                cols = pl.ds(j * chunk, chunk)
                term = scale * dot3(left, (split_p[j, 0], split_p[j, 1]), ((1,), (0,)))
                if first:
                    qgrad[part, cols] = term
                else:
                    qgrad[part, cols] += term

    def group_query_grad(g):
        arrived(weights_in.at[g], w_recv.at[g])
        wait_slab(g)
        add_query_grad(weights_in.at[g], [slab.at[g, j] for j in range(ratio)], False)

    def wait_slab(g):
        for j in range(ratio):
            for h in range(2):
                arrived(slab.at[g, j, halves[h]], slab_recv.at[g, j, h])

    def same_core_query_grad(i):
        g = lax.rem(x + i, nx) * 2 + core
        wait_slab(g)
        add_query_grad(weights_in.at[g], [slab.at[g, j] for j in range(ratio)], False)

    z_step(nz - 1)
    add_query_grad(scores, [feats.at[ga * ratio + j] for j in range(ratio)], True)
    group_query_grad(sibling)
    for s in range(nz - 2, 0, -1):
        z_step(s)
    for i in range(1, nx):
        g = lax.rem(x + i, nx) * 2 + core
        arrived(weights_in.at[g], w_recv.at[g])
        w_forward(i).start()
    for i in range(1, nx):
        same_core_query_grad(i)
    for i in range(1, nx - 1):
        group_query_grad(lax.rem(x + i, nx) * 2 + 1 - core)
    out_copy = pltpu.make_async_copy(qgrad, qgrad_hbm, out_sem.at[0])
    out_copy.start()

    last = lax.rem(x + nx - 1, nx) * 2 + 1 - core
    arrived(weights_in.at[last], w_recv.at[last])
    w_out_copy = pltpu.make_async_copy(weights_in.at[last], w_out, out_sem.at[1])
    w_out_copy.start()
    wait_slab(last)
    slab_out_copy = pltpu.make_async_copy(slab.at[last], slab_out, out_sem.at[2])
    slab_out_copy.start()

    for h in range(2):
        for d in (1, -1):

            @pl.when(inside(z - d, nz))
            def _(d=d, h=h):
                z_sum(z, d, h)

        y_gather(z, h)

    pgrad_ref[...] = partial[me]

    @pl.loop(0, n_pb)
    def _(k):
        zz = k // ny
        yy = k % ny
        for h in range(2):
            when_sent(k // ratio != ga, lambda: slab_feature(k, h))
        for h in range(2):
            far = jnp.abs(zz - z) != 1 if near and h == 1 else True
            unsent = zz == z if near else True
            for d in (1, -1):
                behind = zz <= z if d > 0 else zz >= z
                ahead = zz > z if d > 0 else zz < z
                line = yy == y
                when_sent(
                    jnp.logical_and(jnp.logical_and(line, behind), inside(z + d, nz)),
                    lambda d=d: z_feature(k, h, d),
                )
                when_sent(jnp.logical_and(line, ahead), lambda d=d: z_partial(zz, d, h))
            for e in (1, -1):
                behind = yy <= y if e > 0 else yy >= y
                ahead = yy > y if e > 0 else yy < y
                when_sent(
                    jnp.logical_and(far, jnp.logical_and(behind, inside(y + e, ny))),
                    lambda e=e: y_feature(k, h, e),
                )
                when_sent(jnp.logical_and(unsent, ahead), lambda e=e: y_partial(zz, yy, e, h))

    if near:
        for d in (1, -1):
            when_sent(inside(z + d, nz), lambda d=d: near_feature(d))
            when_sent(inside(z + d, nz), lambda d=d: near_partial(d))
    for i in range(1, n_pa):
        stat_copy(i).wait_send()
    for i in range(nx):
        w_copy(i).wait_send()
    for i in range(1, nx):
        w_forward(i).wait_send()
    out_copy.wait()
    w_out_copy.wait()
    slab_out_copy.wait()


def last_kernel(scale, so_far, weights, slab, out, split_p):
    ratio, _, chunk = slab.shape

    @pl.when(pl.program_id(0) == 0)
    def _():
        for j in range(ratio):
            high, low = split(slab[j])
            split_p[j, 0] = high
            split_p[j, 1] = low

    left = split(weights[...].T)
    for j in range(ratio):
        cols = pl.ds(j * chunk, chunk)
        term = dot3(left, (split_p[j, 0], split_p[j, 1]), ((1,), (0,)))
        out[:, cols] = so_far[:, cols] + scale * term


def body(n_pb, n_pa, queries, passages, pairs, positives):
    rows, width = queries.shape
    group_rows, chunk = passages.shape
    nx = n_pa // 2
    ny = nx
    nz = n_pb // ny
    ratio = n_pb // n_pa
    dma = pltpu.SemaphoreType.DMA
    losses, most, passage_grad, weights, slab = pl.pallas_call(
        functools.partial(kernel, n_pb, n_pa, math.sqrt(width)),
        out_shape=(
            jax.ShapeDtypeStruct((1, rows), F32),
            jax.ShapeDtypeStruct((rows, ratio * chunk), F32),
            jax.ShapeDtypeStruct((group_rows, chunk), F32),
            jax.ShapeDtypeStruct((group_rows, rows), F32),
            jax.ShapeDtypeStruct((ratio, group_rows, chunk), F32),
        ),
        in_specs=[
            pl.BlockSpec(memory_space=pl.ANY),
            pl.BlockSpec(memory_space=pl.ANY),
            pl.BlockSpec(memory_space=pltpu.VMEM),
            pl.BlockSpec(memory_space=pltpu.VMEM),
        ],
        out_specs=(
            pl.BlockSpec(memory_space=pltpu.VMEM),
            pl.BlockSpec(memory_space=pl.ANY),
            pl.BlockSpec(memory_space=pltpu.VMEM),
            pl.BlockSpec(memory_space=pl.ANY),
            pl.BlockSpec(memory_space=pl.ANY),
        ),
        scratch_shapes=[
            pltpu.VMEM((2, rows, chunk), F32),
            pltpu.VMEM((n_pb, rows, chunk), BF16),
            pltpu.VMEM((n_pb, rows, chunk), BF16),
            pltpu.VMEM((n_pb, group_rows, chunk), F32),
            pltpu.VMEM((n_pa, ratio, group_rows, chunk), F32),
            pltpu.VMEM((group_rows, rows), F32),
            pltpu.VMEM((n_pa, group_rows, rows), F32),
            pltpu.VMEM((n_pa, 8, rows), F32),
            pltpu.VMEM((n_pb, group_rows, chunk), F32),
            pltpu.VMEM((nz, ny - 1, group_rows, chunk), F32),
            pltpu.VMEM((nz, ny - 1, group_rows, chunk), F32),
            pltpu.VMEM((2, group_rows // 2, chunk), F32),
            pltpu.VMEM((nz - 1, group_rows, chunk), F32),
            pltpu.VMEM((nz - 1, group_rows, chunk), F32),
            pltpu.VMEM((rows, ratio * chunk), F32),
            pltpu.VMEM((2, group_rows, rows), BF16),
            pltpu.VMEM((ratio, 2, group_rows, chunk), BF16),
            dma((2,)),
            dma,
            dma((3,)),
            dma((n_pb, 2)),
            dma((2, n_pb, 2)),
            dma((2, n_pb, 2)),
            dma((2,)),
            dma((n_pb, 2)),
            dma((n_pa, ratio, 2)),
            dma((n_pa - 1,)),
            dma((n_pa,)),
            dma((nx,)),
            dma((nx,)),
            dma((n_pa,)),
            dma((2, n_pb, 2)),
            dma((2, nz, ny - 1, 2)),
            dma((2,)),
            dma((2,)),
            dma((2, nz, 2)),
            dma((2, nz - 1, 2)),
        ],
        compiler_params=pltpu.CompilerParams(
            collective_id=0, has_side_effects=True, vmem_limit_bytes=62 * 2**20
        ),
    )(queries, passages, pairs.T, positives.reshape(1, rows))
    tile_spec = pl.BlockSpec((TILE, ratio * chunk), lambda t: (t, 0))
    query_grad = pl.pallas_call(
        functools.partial(last_kernel, math.sqrt(width)),
        grid=(rows // TILE,),
        out_shape=jax.ShapeDtypeStruct((rows, ratio * chunk), F32),
        in_specs=[
            tile_spec,
            pl.BlockSpec((group_rows, TILE), lambda t: (0, t)),
            pl.BlockSpec((ratio, group_rows, chunk), lambda t: (0, 0, 0)),
        ],
        out_specs=tile_spec,
        scratch_shapes=[pltpu.VMEM((ratio, 2, group_rows, chunk), BF16)],
        compiler_params=pltpu.CompilerParams(vmem_limit_bytes=62 * 2**20),
    )(most, weights, slab)
    return losses.reshape(-1), query_grad, passage_grad


def solution(mesh):
    in_specs = (P("pb", None), P("pa", "pb"), P("pb", None), P("pb"))
    out_specs = (P("pb"), P("pb", "pa"), P("pa", "pb"))
    return jax.shard_map(
        functools.partial(body, mesh.shape["pb"], mesh.shape["pa"]),
        mesh=mesh,
        in_specs=in_specs,
        out_specs=out_specs,
        check_vma=False,
    )
```

```python
import functools
import math

import jax
import jax.numpy as jnp
from jax import lax
from jax.experimental import pallas as pl
from jax.experimental.pallas import tpu as pltpu
from jax.sharding import PartitionSpec as P

BLK = 256
TILE = 256
low_value = -1e30
MESH = pl.DeviceIdType.MESH
F32 = jnp.float32
BF16 = jnp.bfloat16


def split(value):
    high = value.astype(BF16)
    return high, (value - high.astype(F32)).astype(BF16)


def dot3(left, right, dims):
    def one(a, b):
        return lax.dot_general(a, b, (dims, ((), ())), preferred_element_type=F32)

    return one(left[0], right[1]) + one(left[1], right[0]) + one(left[0], right[0])


def kernel(
    n_pb,
    n_pa,
    scale,
    q_hbm,
    p_hbm,
    pairs_ref,
    pos_ref,
    losses_ref,
    qgrad_hbm,
    pgrad_ref,
    w_out,
    slab_out,
    qstage,
    qhi,
    qlo,
    feats,
    slab,
    scores,
    weights_in,
    stats,
    partial,
    y_up,
    y_down,
    near_in,
    z_up,
    z_down,
    qgrad,
    split_w,
    split_p,
    q_sem,
    own_sem,
    out_sem,
    feat_recv,
    zf_send,
    yf_send,
    near_send,
    slab_send,
    slab_recv,
    relay_send,
    stat_send,
    stat_recv,
    w_send,
    w_pass,
    w_recv,
    yr_send,
    y_recv,
    near_out,
    near_recv,
    zr_send,
    z_recv,
):
    nx = n_pa // 2
    ny = nx
    nz = n_pb // ny
    ratio = n_pb // n_pa
    rows = q_hbm.shape[0]
    chunk = p_hbm.shape[1]
    group_rows = p_hbm.shape[0]
    half = group_rows // 2
    halves = [pl.ds(h * half, half) for h in range(2)]
    near = ny == 2 and nz == 4
    q_blocks = rows // BLK
    p_blocks = group_rows // BLK

    me = lax.axis_index("pb")
    ga = lax.axis_index("pa")
    z = me // ny
    y = me % ny
    x = ga // 2
    core = ga % 2
    sibling = x * 2 + 1 - core

    def inside(value, size):
        return jnp.logical_and(value >= 0, value < size)

    def remote(src, dst, send_sem, recv_sem, **where):
        return pltpu.make_async_remote_copy(
            src_ref=src,
            dst_ref=dst,
            send_sem=send_sem,
            recv_sem=recv_sem,
            device_id=where,
            device_id_type=MESH,
        )

    def arrived(buffer, sem):
        remote(buffer, buffer, own_sem, sem, pa=sibling).wait_recv()

    def q_copy(k):
        start = pl.multiple_of(k * chunk, chunk)
        slot = lax.rem(k, 2)
        return pltpu.make_async_copy(
            q_hbm.at[:, pl.ds(start, chunk)], qstage.at[slot], q_sem.at[slot]
        )

    own_copy = pltpu.make_async_copy(p_hbm, feats.at[me], own_sem)
    own_copy.start()
    q_copy(jnp.int32(0)).start()
    q_copy(jnp.int32(1)).start()

    barrier = pltpu.get_barrier_semaphore()
    greeted = jnp.int32(n_pa - 1)
    for step in (1, -1):
        for valid, target in (
            (inside(z + step, nz), (z + step) * ny + y),
            (inside(y + step, ny), z * ny + y + step),
        ):

            @pl.when(valid)
            def _(target=target):
                pl.semaphore_signal(barrier, inc=1, device_id={"pb": target}, device_id_type=MESH)

            greeted = greeted + valid.astype(jnp.int32)
    for i in range(1, n_pa):
        pl.semaphore_signal(
            barrier, inc=1, device_id={"pa": lax.rem(ga + i, n_pa)}, device_id_type=MESH
        )
    pl.semaphore_wait(barrier, greeted)
    own_copy.wait()

    def feature(k, h, send_sem, **where):
        ref = feats.at[k, halves[h]]
        return remote(ref, ref, send_sem, feat_recv.at[k, h], **where)

    def z_feature(k, h, d):
        way = 0 if d > 0 else 1
        return feature(k, h, zf_send.at[way, k, h], pb=(z + d) * ny + y)

    def y_feature(k, h, e):
        way = 0 if e > 0 else 1
        return feature(k, h, yf_send.at[way, k, h], pb=z * ny + y + e)

    def near_feature(d):
        way = 0 if d > 0 else 1
        return feature(z * ny + 1 - y, 1, near_send.at[way], pb=(z + d) * ny + y)

    def feature_arrived(k, h):
        arrived(feats.at[k, halves[h]], feat_recv.at[k, h])

    def slab_feature(k, h):
        return remote(
            feats.at[k, halves[h]],
            slab.at[ga, k % ratio, halves[h]],
            slab_send.at[k, h],
            slab_recv.at[ga, k % ratio, h],
            pa=k // ratio,
        )

    def late(side):
        return jnp.where(side == 1, z < nz // 2, z >= nz // 2)

    relay_way = jnp.where(x == 1, -1, 1)
    relay_first = z == jnp.where(x == 1, nz // 2, nz // 2 - 1)
    relay_next = jnp.logical_and(late(x), inside(z + relay_way, nz))
    relays = jnp.logical_or(relay_first, relay_next)

    def relay_copy(i):
        g = (1 - x) * 2 + i
        ref = slab.at[g, y, halves[1]]
        target = (z + relay_way) * ny + y
        return remote(ref, ref, relay_send.at[i], slab_recv.at[g, y, 1], pb=target)

    def relay(valid):
        @pl.when(valid)
        def _():
            for i in range(2):
                g = (1 - x) * 2 + i
                arrived(slab.at[g, y, halves[1]], slab_recv.at[g, y, 1])
                relay_copy(i).start()

    def slab_needed(k, h):
        needed = k // ratio != ga
        if near and h == 1:
            side = k // ratio // 2
            handed = jnp.logical_and(jnp.logical_and(side != x, late(side)), k % ny == y)
            needed = jnp.logical_and(needed, jnp.logical_not(handed))
        return needed

    def when_start(valid, make):
        @pl.when(valid)
        def _():
            make().start()

    def when_sent(valid, make):
        @pl.when(valid)
        def _():
            make().wait_send()

    def send_own(h):
        for d in (1, -1):
            when_start(inside(z + d, nz), lambda d=d: z_feature(me, h, d))
        for e in (1, -1):
            when_start(inside(y + e, ny), lambda e=e: y_feature(me, h, e))

    send_own(0)
    for h in range(2):
        when_start(slab_needed(me, h), lambda: slab_feature(me, h))

    @pl.loop(0, n_pb)
    def _(k):
        q_copy(k).wait()
        slot = lax.rem(k, 2)

        @pl.loop(0, rows // 128)
        def _(t):
            part = pl.ds(pl.multiple_of(t * 128, 128), 128)
            high, low = split(qstage[slot, part, :])
            qhi[k, part, :] = high
            qlo[k, part, :] = low

        @pl.when(k + 2 < n_pb)
        def _():
            q_copy(k + 2).start()

        @pl.when(k == n_pb // 2)
        def _():
            send_own(1)

    scores[...] = jnp.zeros_like(scores)

    def add_scores(k):
        high, low = split(feats[k])

        @pl.loop(0, rows // TILE)
        def _(t):
            part = pl.ds(pl.multiple_of(t * TILE, TILE), TILE)
            scores[:, part] += dot3(
                (high, low), (qhi[k, part, :], qlo[k, part, :]), ((1,), (1,))
            )

    add_scores(me)

    def y_round(r, parts, score):
        for d in (1, -1):
            zz = z + d * r
            once = inside(zz, nz) if d > 0 else jnp.logical_and(inside(zz, nz), r > 0)
            for t in range(1, ny):
                for e in (1, -1):
                    yy = y + e * t
                    k = zz * ny + yy

                    @pl.when(jnp.logical_and(once, inside(yy, ny)))
                    def _(k=k, e=e):
                        for h in parts:
                            feature_arrived(k, h)
                            when_start(inside(y - e, ny), lambda: y_feature(k, h, -e))
                            when_start(slab_needed(k, h), lambda: slab_feature(k, h))
                        if score:
                            add_scores(k)

    @pl.loop(1, nz)
    def _(s):
        for h in range(2):
            for d in (1, -1):
                zz = z + d * s
                k = zz * ny + y

                @pl.when(inside(zz, nz))
                def _(k=k, d=d, h=h):
                    feature_arrived(k, h)
                    when_start(inside(z - d, nz), lambda: z_feature(k, h, -d))
                    for e in (1, -1):
                        whole = s > 1 if near and h == 1 else True
                        when_start(
                            jnp.logical_and(whole, inside(y + e, ny)),
                            lambda e=e: y_feature(k, h, e),
                        )
                    when_start(slab_needed(k, h), lambda: slab_feature(k, h))

        if near:
            for d in (1, -1):
                when_start(
                    jnp.logical_and(s == nz - 2, inside(z + d, nz)), lambda d=d: near_feature(d)
                )

        for d in (1, -1):
            zz = z + d * s

            @pl.when(inside(zz, nz))
            def _(zz=zz):
                add_scores(zz * ny + y)

        @pl.when(s == 1)
        def _():
            y_round(jnp.int32(0), (0, 1), True)

        @pl.when(s > 1)
        def _():
            y_round(s - 1, (0,), False)

    y_round(nz - 1, (0,), False)

    @pl.loop(0, nz - 1)
    def _(i):
        y_round(jnp.where(i < nz - 2, i + 2, 1), (1,), True)

    q_first = me * q_blocks
    lane_block = lax.broadcasted_iota(jnp.int32, (1, rows), 1) // BLK

    def live_lanes(p_block):
        found = jnp.zeros((1, rows), jnp.int32)
        for r in range(pairs_ref.shape[1]):
            same = jnp.logical_and(
                pairs_ref[0:1, r : r + 1] - q_first == lane_block,
                pairs_ref[1:2, r : r + 1] == ga * p_blocks + p_block,
            )
            found = found + same.astype(jnp.int32)
        return found > 0

    live = [live_lanes(b) for b in range(p_blocks)]
    row_ids = lax.broadcasted_iota(jnp.int32, (BLK, rows), 0)

    def positive_mask(b):
        return row_ids == pos_ref[...] - (ga * p_blocks + b) * BLK

    tops, totals, hits = [], [], []
    for b in range(p_blocks):
        tile = scores[b * BLK : (b + 1) * BLK, :] * scale
        scores[b * BLK : (b + 1) * BLK, :] = tile
        top = jnp.max(tile, axis=0, keepdims=True)
        total = jnp.sum(jnp.exp(tile - top), axis=0, keepdims=True)
        tops.append(jnp.where(live[b], top, low_value))
        totals.append(jnp.where(live[b], total, 0.0))
        hits.append(jnp.sum(jnp.where(positive_mask(b), tile, 0.0), axis=0, keepdims=True))

    def merge(tops, totals):
        joint = functools.reduce(jnp.maximum, tops)
        return joint, sum(t * jnp.exp(m - joint) for m, t in zip(tops, totals))

    top, total = merge(tops, totals)
    stats[ga, 0:1, :] = top
    stats[ga, 1:2, :] = total
    stats[ga, 2:3, :] = sum(hits)
    stats[ga, 3:8, :] = jnp.zeros((5, rows), F32)

    def stat_copy(i):
        return remote(
            stats.at[ga],
            stats.at[ga],
            stat_send.at[i - 1],
            stat_recv.at[ga],
            pa=lax.rem(ga + i, n_pa),
        )

    for i in range(1, n_pa):
        stat_copy(i).start()
    for i in range(1, n_pa):
        other = lax.rem(ga + i, n_pa)
        arrived(stats.at[other], stat_recv.at[other])
    joint, total = merge(
        [stats[g, 0:1, :] for g in range(n_pa)], [stats[g, 1:2, :] for g in range(n_pa)]
    )
    log_norm = joint + jnp.log(total)
    losses_ref[...] = log_norm - sum(stats[g, 2:3, :] for g in range(n_pa))

    for b in range(p_blocks):
        tile = scores[b * BLK : (b + 1) * BLK, :]
        soft = jnp.where(live[b], jnp.exp(tile - log_norm), 0.0)
        weight = soft - positive_mask(b).astype(F32)
        scores[b * BLK : (b + 1) * BLK, :] = weight
        high, low = split(weight)
        split_w[0, b * BLK : (b + 1) * BLK, :] = high
        split_w[1, b * BLK : (b + 1) * BLK, :] = low

    def w_copy(i):
        target = lax.rem(x + i, nx) * 2 + core if i else sibling
        return remote(scores, weights_in.at[ga], w_send.at[i], w_recv.at[ga], pa=target)

    def w_forward(i):
        g = lax.rem(x + i, nx) * 2 + core
        return remote(weights_in.at[g], weights_in.at[g], w_pass.at[i], w_recv.at[g], pa=sibling)

    for i in range(nx):
        w_copy(i).start()
    if near:
        relay(relay_first)

    def form_partial(k):
        left = (split_w[0], split_w[1])
        for n in range(0, chunk, TILE):
            part = pl.ds(n, TILE)
            partial[k, :, part] = scale * dot3(
                left, (qhi[k, :, part], qlo[k, :, part]), ((1,), (0,))
            )

    def y_slot(zz, yy, e, h):
        return y_up.at[zz, yy - 1, halves[h]] if e > 0 else y_down.at[zz, yy, halves[h]]

    def y_sem(zz, yy, e, h):
        return y_recv.at[0 if e > 0 else 1, zz, yy - 1 if e > 0 else yy, h]

    def add_partial(k, h, slot, sem):
        arrived(slot, sem)
        partial[k, halves[h]] += slot[...]

    def y_sum(zz, yy, e, h):
        add_partial(zz * ny + yy, h, y_slot(zz, yy, e, h), y_sem(zz, yy, e, h))

    def y_partial(zz, yy, e, h):
        way = 0 if e > 0 else 1
        k = zz * ny + yy
        return remote(
            partial.at[k, halves[h]],
            y_slot(zz, yy, e, h),
            yr_send.at[way, k, h],
            y_sem(zz, yy, e, h),
            pb=z * ny + y + e,
        )

    def near_partial(d):
        way = 0 if d > 0 else 1
        return remote(
            partial.at[(z + d) * ny + 1 - y, halves[1]],
            near_in.at[way],
            near_out.at[way],
            near_recv.at[way],
            pb=(z + d) * ny + y,
        )

    def each_z(body, last):
        @pl.loop(0, nz - last)
        def _(i):
            s = nz - 1 - i
            for d in (1, -1):
                zz = z + d * s
                valid = inside(zz, nz) if d > 0 else jnp.logical_and(inside(zz, nz), s > 0)

                @pl.when(valid)
                def _(zz=zz, d=d):
                    body(zz, d, s)

    across = 1 - y
    farthest = jnp.maximum(z, nz - 1 - z)

    def across_each(s, act):
        for d in (1, -1) if not (isinstance(s, int) and s == 0) else (1,):
            for e in (1, -1):
                zz = z + d * s

                @pl.when(jnp.logical_and(inside(zz, nz), inside(y + e, ny)))
                def _(zz=zz, e=e):
                    act(zz, e)

    def across_start(s, h):
        across_each(s, lambda zz, e: y_partial(zz, across, e, h).start())

    def across_sent(s, h):
        across_each(s, lambda zz, e: y_partial(zz, across, e, h).wait_send())

    if near:
        def form_across(zz, d, s):
            form_partial(zz * ny + across)
            when_start(s == 1, lambda: near_partial(d))

            @pl.when(s == farthest)
            def _():
                for e in (1, -1):
                    when_start(inside(y + e, ny), lambda e=e: y_partial(zz, across, e, 0))

        each_z(form_across, 0)
        across_start(farthest, 1)
    else:
        for t in range(ny - 1, 0, -1):
            for e in (1, -1):
                yy = y + e * t

                @pl.when(inside(yy, ny))
                def _(yy=yy, e=e):
                    def send_one(zz, d, s):
                        form_partial(zz * ny + yy)
                        for h in range(2):

                            @pl.when(inside(y - e, ny))
                            def _(h=h):
                                y_sum(zz, yy, e, h)

                            y_partial(zz, yy, e, h).start()

                    each_z(send_one, 0)

    each_z(lambda zz, d, s: form_partial(zz * ny + y), 0)

    def across_next(s, h):
        if s > 1 or h == 0:

            @pl.when(farthest >= s)
            def _():
                across_sent(s, h)
                if s > 2 or h == 0:
                    across_start(s - 1, h)

        if s == 1 and h == 1:
            for d in (1, -1):
                way = 0 if d > 0 else 1

                @pl.when(inside(z - d, nz))
                def _(way=way):
                    add_partial(z * ny + across, 1, near_in.at[way], near_recv.at[way])

            across_start(0, 1)

    def z_slot(zz, d, h):
        return z_up.at[zz - 1, halves[h]] if d > 0 else z_down.at[zz, halves[h]]

    def z_sem(zz, d, h):
        return z_recv.at[0 if d > 0 else 1, zz - 1 if d > 0 else zz, h]

    def z_partial(zz, d, h):
        way = 0 if d > 0 else 1
        return remote(
            partial.at[zz * ny + y, halves[h]],
            z_slot(zz, d, h),
            zr_send.at[way, zz, h],
            z_sem(zz, d, h),
            pb=(z + d) * ny + y,
        )

    def y_gather(zz, h):
        for e in (1, -1):

            @pl.when(inside(y - e, ny))
            def _(e=e):
                y_sum(zz, y, e, h)

    def z_sum(zz, d, h):
        add_partial(zz * ny + y, h, z_slot(zz, d, h), z_sem(zz, d, h))

    def z_step(s):
        for h in range(2):
            if near:
                across_next(s, h)
            for d in (1, -1):
                zz = z + d * s

                @pl.when(inside(zz, nz))
                def _(zz=zz, d=d, h=h):
                    if not (near and s == 1 and h == 1):
                        y_gather(zz, h)

                    @pl.when(inside(z - d, nz))
                    def _():
                        z_sum(zz, d, h)

                    z_partial(zz, d, h).start()

    def add_query_grad(w_ref, p_refs, first):
        for j in range(ratio):
            high, low = split(p_refs[j][...])
            split_p[j, 0] = high
            split_p[j, 1] = low

        @pl.loop(0, rows // TILE)
        def _(t):
            part = pl.ds(pl.multiple_of(t * TILE, TILE), TILE)
            left = split(w_ref[:, part].T)
            for j in range(ratio):
                cols = pl.ds(j * chunk, chunk)
                term = scale * dot3(left, (split_p[j, 0], split_p[j, 1]), ((1,), (0,)))
                if first:
                    qgrad[part, cols] = term
                else:
                    qgrad[part, cols] += term

    def group_query_grad(g):
        arrived(weights_in.at[g], w_recv.at[g])
        wait_slab(g)
        add_query_grad(weights_in.at[g], [slab.at[g, j] for j in range(ratio)], False)

    def wait_slab(g):
        for j in range(ratio):
            for h in range(2):
                waited = False
                if near and h == 1:
                    waited = jnp.logical_and(jnp.logical_and(relays, g // 2 != x), y == j)

                @pl.when(jnp.logical_not(waited))
                def _(j=j, h=h):
                    arrived(slab.at[g, j, halves[h]], slab_recv.at[g, j, h])

    def same_core_query_grad(i):
        g = lax.rem(x + i, nx) * 2 + core
        wait_slab(g)
        add_query_grad(weights_in.at[g], [slab.at[g, j] for j in range(ratio)], False)

    z_step(nz - 1)
    add_query_grad(scores, [feats.at[ga * ratio + j] for j in range(ratio)], True)
    group_query_grad(sibling)
    for s in range(nz - 2, 0, -1):
        z_step(s)
        if near and s == nz - 2:
            relay(relay_next)
    for i in range(1, nx):
        g = lax.rem(x + i, nx) * 2 + core
        arrived(weights_in.at[g], w_recv.at[g])
        w_forward(i).start()
    for i in range(1, nx):
        same_core_query_grad(i)
    for i in range(1, nx - 1):
        group_query_grad(lax.rem(x + i, nx) * 2 + 1 - core)
    out_copy = pltpu.make_async_copy(qgrad, qgrad_hbm, out_sem.at[0])
    out_copy.start()

    last = lax.rem(x + nx - 1, nx) * 2 + 1 - core
    arrived(weights_in.at[last], w_recv.at[last])
    w_out_copy = pltpu.make_async_copy(weights_in.at[last], w_out, out_sem.at[1])
    w_out_copy.start()
    wait_slab(last)
    slab_out_copy = pltpu.make_async_copy(slab.at[last], slab_out, out_sem.at[2])
    slab_out_copy.start()

    for h in range(2):
        for d in (1, -1):

            @pl.when(inside(z - d, nz))
            def _(d=d, h=h):
                z_sum(z, d, h)

        y_gather(z, h)

    pgrad_ref[...] = partial[me]

    @pl.loop(0, n_pb)
    def _(k):
        zz = k // ny
        yy = k % ny
        for h in range(2):
            when_sent(slab_needed(k, h), lambda: slab_feature(k, h))
        for h in range(2):
            far = jnp.abs(zz - z) != 1 if near and h == 1 else True
            unsent = zz == z if near else True
            for d in (1, -1):
                behind = zz <= z if d > 0 else zz >= z
                ahead = zz > z if d > 0 else zz < z
                line = yy == y
                when_sent(
                    jnp.logical_and(jnp.logical_and(line, behind), inside(z + d, nz)),
                    lambda d=d: z_feature(k, h, d),
                )
                when_sent(jnp.logical_and(line, ahead), lambda d=d: z_partial(zz, d, h))
            for e in (1, -1):
                behind = yy <= y if e > 0 else yy >= y
                ahead = yy > y if e > 0 else yy < y
                when_sent(
                    jnp.logical_and(far, jnp.logical_and(behind, inside(y + e, ny))),
                    lambda e=e: y_feature(k, h, e),
                )
                when_sent(jnp.logical_and(unsent, ahead), lambda e=e: y_partial(zz, yy, e, h))

    if near:
        for i in range(2):
            when_sent(relays, lambda i=i: relay_copy(i))
        for d in (1, -1):
            when_sent(inside(z + d, nz), lambda d=d: near_feature(d))
            when_sent(inside(z + d, nz), lambda d=d: near_partial(d))
    for i in range(1, n_pa):
        stat_copy(i).wait_send()
    for i in range(nx):
        w_copy(i).wait_send()
    for i in range(1, nx):
        w_forward(i).wait_send()
    out_copy.wait()
    w_out_copy.wait()
    slab_out_copy.wait()


def last_kernel(scale, so_far, weights, slab, out, split_p):
    ratio, _, chunk = slab.shape

    @pl.when(pl.program_id(0) == 0)
    def _():
        for j in range(ratio):
            high, low = split(slab[j])
            split_p[j, 0] = high
            split_p[j, 1] = low

    left = split(weights[...].T)
    for j in range(ratio):
        cols = pl.ds(j * chunk, chunk)
        term = dot3(left, (split_p[j, 0], split_p[j, 1]), ((1,), (0,)))
        out[:, cols] = so_far[:, cols] + scale * term


def body(n_pb, n_pa, queries, passages, pairs, positives):
    rows, width = queries.shape
    group_rows, chunk = passages.shape
    nx = n_pa // 2
    ny = nx
    nz = n_pb // ny
    ratio = n_pb // n_pa
    dma = pltpu.SemaphoreType.DMA
    losses, most, passage_grad, weights, slab = pl.pallas_call(
        functools.partial(kernel, n_pb, n_pa, math.sqrt(width)),
        out_shape=(
            jax.ShapeDtypeStruct((1, rows), F32),
            jax.ShapeDtypeStruct((rows, ratio * chunk), F32),
            jax.ShapeDtypeStruct((group_rows, chunk), F32),
            jax.ShapeDtypeStruct((group_rows, rows), F32),
            jax.ShapeDtypeStruct((ratio, group_rows, chunk), F32),
        ),
        in_specs=[
            pl.BlockSpec(memory_space=pl.ANY),
            pl.BlockSpec(memory_space=pl.ANY),
            pl.BlockSpec(memory_space=pltpu.VMEM),
            pl.BlockSpec(memory_space=pltpu.VMEM),
        ],
        out_specs=(
            pl.BlockSpec(memory_space=pltpu.VMEM),
            pl.BlockSpec(memory_space=pl.ANY),
            pl.BlockSpec(memory_space=pltpu.VMEM),
            pl.BlockSpec(memory_space=pl.ANY),
            pl.BlockSpec(memory_space=pl.ANY),
        ),
        scratch_shapes=[
            pltpu.VMEM((2, rows, chunk), F32),
            pltpu.VMEM((n_pb, rows, chunk), BF16),
            pltpu.VMEM((n_pb, rows, chunk), BF16),
            pltpu.VMEM((n_pb, group_rows, chunk), F32),
            pltpu.VMEM((n_pa, ratio, group_rows, chunk), F32),
            pltpu.VMEM((group_rows, rows), F32),
            pltpu.VMEM((n_pa, group_rows, rows), F32),
            pltpu.VMEM((n_pa, 8, rows), F32),
            pltpu.VMEM((n_pb, group_rows, chunk), F32),
            pltpu.VMEM((nz, ny - 1, group_rows, chunk), F32),
            pltpu.VMEM((nz, ny - 1, group_rows, chunk), F32),
            pltpu.VMEM((2, group_rows // 2, chunk), F32),
            pltpu.VMEM((nz - 1, group_rows, chunk), F32),
            pltpu.VMEM((nz - 1, group_rows, chunk), F32),
            pltpu.VMEM((rows, ratio * chunk), F32),
            pltpu.VMEM((2, group_rows, rows), BF16),
            pltpu.VMEM((ratio, 2, group_rows, chunk), BF16),
            dma((2,)),
            dma,
            dma((3,)),
            dma((n_pb, 2)),
            dma((2, n_pb, 2)),
            dma((2, n_pb, 2)),
            dma((2,)),
            dma((n_pb, 2)),
            dma((n_pa, ratio, 2)),
            dma((2,)),
            dma((n_pa - 1,)),
            dma((n_pa,)),
            dma((nx,)),
            dma((nx,)),
            dma((n_pa,)),
            dma((2, n_pb, 2)),
            dma((2, nz, ny - 1, 2)),
            dma((2,)),
            dma((2,)),
            dma((2, nz, 2)),
            dma((2, nz - 1, 2)),
        ],
        compiler_params=pltpu.CompilerParams(
            collective_id=0, has_side_effects=True, vmem_limit_bytes=62 * 2**20
        ),
    )(queries, passages, pairs.T, positives.reshape(1, rows))
    tile_spec = pl.BlockSpec((TILE, ratio * chunk), lambda t: (t, 0))
    query_grad = pl.pallas_call(
        functools.partial(last_kernel, math.sqrt(width)),
        grid=(rows // TILE,),
        out_shape=jax.ShapeDtypeStruct((rows, ratio * chunk), F32),
        in_specs=[
            tile_spec,
            pl.BlockSpec((group_rows, TILE), lambda t: (0, t)),
            pl.BlockSpec((ratio, group_rows, chunk), lambda t: (0, 0, 0)),
        ],
        out_specs=tile_spec,
        scratch_shapes=[pltpu.VMEM((ratio, 2, group_rows, chunk), BF16)],
        compiler_params=pltpu.CompilerParams(vmem_limit_bytes=62 * 2**20),
    )(most, weights, slab)
    return losses.reshape(-1), query_grad, passage_grad


def solution(mesh):
    in_specs = (P("pb", None), P("pa", "pb"), P("pb", None), P("pb"))
    out_specs = (P("pb"), P("pb", "pa"), P("pa", "pb"))
    return jax.shard_map(
        functools.partial(body, mesh.shape["pb"], mesh.shape["pa"]),
        mesh=mesh,
        in_specs=in_specs,
        out_specs=out_specs,
        check_vma=False,
    )
```

```python
import functools
import math

import jax
import jax.numpy as jnp
from jax import lax
from jax.experimental import pallas as pl
from jax.experimental.pallas import tpu as pltpu
from jax.sharding import PartitionSpec as P

BLK = 256
TILE = 256
low_value = -1e30
MESH = pl.DeviceIdType.MESH
F32 = jnp.float32
BF16 = jnp.bfloat16


def split(value):
    high = value.astype(BF16)
    return high, (value - high.astype(F32)).astype(BF16)


def dot3(left, right, dims):
    def one(a, b):
        return lax.dot_general(a, b, (dims, ((), ())), preferred_element_type=F32)

    return one(left[0], right[1]) + one(left[1], right[0]) + one(left[0], right[0])


def kernel(
    n_pb,
    n_pa,
    scale,
    q_hbm,
    p_hbm,
    pairs_ref,
    pos_ref,
    losses_ref,
    qgrad_hbm,
    pgrad_ref,
    w_out,
    slab_out,
    qstage,
    qhi,
    qlo,
    feats,
    slab,
    scores,
    weights_in,
    stats,
    partial,
    y_up,
    y_down,
    near_in,
    z_up,
    z_down,
    qgrad,
    split_w,
    split_p,
    q_sem,
    own_sem,
    out_sem,
    feat_recv,
    zf_send,
    yf_send,
    near_send,
    slab_send,
    slab_recv,
    relay_send,
    stat_send,
    stat_recv,
    w_send,
    w_pass,
    w_recv,
    yr_send,
    y_recv,
    near_out,
    near_recv,
    zr_send,
    z_recv,
):
    nx = n_pa // 2
    ny = nx
    nz = n_pb // ny
    ratio = n_pb // n_pa
    rows = q_hbm.shape[0]
    chunk = p_hbm.shape[1]
    group_rows = p_hbm.shape[0]
    half = group_rows // 2
    halves = [pl.ds(h * half, half) for h in range(2)]
    near = ny == 2 and nz == 4
    q_blocks = rows // BLK
    p_blocks = group_rows // BLK

    me = lax.axis_index("pb")
    ga = lax.axis_index("pa")
    z = me // ny
    y = me % ny
    x = ga // 2
    core = ga % 2
    sibling = x * 2 + 1 - core

    def inside(value, size):
        return jnp.logical_and(value >= 0, value < size)

    def remote(src, dst, send_sem, recv_sem, **where):
        return pltpu.make_async_remote_copy(
            src_ref=src,
            dst_ref=dst,
            send_sem=send_sem,
            recv_sem=recv_sem,
            device_id=where,
            device_id_type=MESH,
        )

    def arrived(buffer, sem):
        remote(buffer, buffer, own_sem, sem, pa=sibling).wait_recv()

    def q_copy(k):
        start = pl.multiple_of(k * chunk, chunk)
        slot = lax.rem(k, 2)
        return pltpu.make_async_copy(
            q_hbm.at[:, pl.ds(start, chunk)], qstage.at[slot], q_sem.at[slot]
        )

    own_copy = pltpu.make_async_copy(p_hbm, feats.at[me], own_sem)
    own_copy.start()
    q_copy(jnp.int32(0)).start()
    q_copy(jnp.int32(1)).start()

    barrier = pltpu.get_barrier_semaphore()
    greeted = jnp.int32(n_pa - 1)
    for step in (1, -1):
        for valid, target in (
            (inside(z + step, nz), (z + step) * ny + y),
            (inside(y + step, ny), z * ny + y + step),
        ):

            @pl.when(valid)
            def _(target=target):
                pl.semaphore_signal(barrier, inc=1, device_id={"pb": target}, device_id_type=MESH)

            greeted = greeted + valid.astype(jnp.int32)
    for i in range(1, n_pa):
        pl.semaphore_signal(
            barrier, inc=1, device_id={"pa": lax.rem(ga + i, n_pa)}, device_id_type=MESH
        )
    pl.semaphore_wait(barrier, greeted)
    own_copy.wait()

    def feature(k, h, send_sem, **where):
        ref = feats.at[k, halves[h]]
        return remote(ref, ref, send_sem, feat_recv.at[k, h], **where)

    def z_feature(k, h, d):
        way = 0 if d > 0 else 1
        return feature(k, h, zf_send.at[way, k, h], pb=(z + d) * ny + y)

    def y_feature(k, h, e):
        way = 0 if e > 0 else 1
        return feature(k, h, yf_send.at[way, k, h], pb=z * ny + y + e)

    def near_feature(d):
        way = 0 if d > 0 else 1
        return feature(z * ny + 1 - y, 1, near_send.at[way], pb=(z + d) * ny + y)

    def feature_arrived(k, h):
        arrived(feats.at[k, halves[h]], feat_recv.at[k, h])

    def slab_feature(k, h):
        return remote(
            feats.at[k, halves[h]],
            slab.at[ga, k % ratio, halves[h]],
            slab_send.at[k, h],
            slab_recv.at[ga, k % ratio, h],
            pa=k // ratio,
        )

    def late(side):
        return jnp.where(side == 1, z < nz // 2, z >= nz // 2)

    relay_way = jnp.where(x == 1, -1, 1)
    relay_first = z == jnp.where(x == 1, nz // 2, nz // 2 - 1)
    relay_next = jnp.logical_and(late(x), inside(z + relay_way, nz))
    relays = jnp.logical_or(relay_first, relay_next)

    def relay_copy(i):
        g = (1 - x) * 2 + i
        ref = slab.at[g, y, halves[1]]
        target = (z + relay_way) * ny + y
        return remote(ref, ref, relay_send.at[i], slab_recv.at[g, y, 1], pb=target)

    def relay(valid):
        @pl.when(valid)
        def _():
            for i in range(2):
                g = (1 - x) * 2 + i
                arrived(slab.at[g, y, halves[1]], slab_recv.at[g, y, 1])
                relay_copy(i).start()

    def slab_needed(k, h):
        needed = k // ratio != ga
        if near and h == 1:
            side = k // ratio // 2
            handed = jnp.logical_and(jnp.logical_and(side != x, late(side)), k % ny == y)
            needed = jnp.logical_and(needed, jnp.logical_not(handed))
        return needed

    def when_start(valid, make):
        @pl.when(valid)
        def _():
            make().start()

    def when_sent(valid, make):
        @pl.when(valid)
        def _():
            make().wait_send()

    def send_own(h):
        for d in (1, -1):
            when_start(inside(z + d, nz), lambda d=d: z_feature(me, h, d))
        for e in (1, -1):
            when_start(inside(y + e, ny), lambda e=e: y_feature(me, h, e))

    send_own(0)
    for h in range(2):
        when_start(slab_needed(me, h), lambda: slab_feature(me, h))

    @pl.loop(0, n_pb)
    def _(k):
        q_copy(k).wait()
        slot = lax.rem(k, 2)

        @pl.loop(0, rows // 128)
        def _(t):
            part = pl.ds(pl.multiple_of(t * 128, 128), 128)
            high, low = split(qstage[slot, part, :])
            qhi[k, part, :] = high
            qlo[k, part, :] = low

        @pl.when(k + 2 < n_pb)
        def _():
            q_copy(k + 2).start()

        @pl.when(k == n_pb // 2)
        def _():
            send_own(1)

    scores[...] = jnp.zeros_like(scores)

    def add_scores(k):
        high, low = split(feats[k])

        @pl.loop(0, rows // TILE)
        def _(t):
            part = pl.ds(pl.multiple_of(t * TILE, TILE), TILE)
            scores[:, part] += dot3(
                (high, low), (qhi[k, part, :], qlo[k, part, :]), ((1,), (1,))
            )

    add_scores(me)

    def y_round(r, parts, score):
        for d in (1, -1):
            zz = z + d * r
            once = inside(zz, nz) if d > 0 else jnp.logical_and(inside(zz, nz), r > 0)
            for t in range(1, ny):
                for e in (1, -1):
                    yy = y + e * t
                    k = zz * ny + yy

                    @pl.when(jnp.logical_and(once, inside(yy, ny)))
                    def _(k=k, e=e):
                        for h in parts:
                            feature_arrived(k, h)
                            when_start(inside(y - e, ny), lambda: y_feature(k, h, -e))
                            now = slab_needed(k, h)
                            if parts == (1,):
                                now = jnp.logical_and(now, k // ratio // 2 == x)
                            when_start(now, lambda: slab_feature(k, h))
                        if score:
                            add_scores(k)

    @pl.loop(1, nz)
    def _(s):
        for h in range(2):
            for d in (1, -1):
                zz = z + d * s
                k = zz * ny + y

                @pl.when(inside(zz, nz))
                def _(k=k, d=d, h=h):
                    feature_arrived(k, h)
                    when_start(inside(z - d, nz), lambda: z_feature(k, h, -d))
                    for e in (1, -1):
                        whole = s > 1 if near and h == 1 else True
                        when_start(
                            jnp.logical_and(whole, inside(y + e, ny)),
                            lambda e=e: y_feature(k, h, e),
                        )
                    when_start(slab_needed(k, h), lambda: slab_feature(k, h))

        if near:
            for d in (1, -1):
                when_start(
                    jnp.logical_and(s == nz - 2, inside(z + d, nz)), lambda d=d: near_feature(d)
                )

        for d in (1, -1):
            zz = z + d * s

            @pl.when(inside(zz, nz))
            def _(zz=zz):
                add_scores(zz * ny + y)

        @pl.when(s == 1)
        def _():
            y_round(jnp.int32(0), (0, 1), True)

        @pl.when(s > 1)
        def _():
            y_round(s - 1, (0,), False)

    y_round(nz - 1, (0,), False)

    @pl.loop(0, nz - 1)
    def _(i):
        y_round(jnp.where(i < nz - 2, i + 2, 1), (1,), True)

    q_first = me * q_blocks
    lane_block = lax.broadcasted_iota(jnp.int32, (1, rows), 1) // BLK

    def live_lanes(p_block):
        found = jnp.zeros((1, rows), jnp.int32)
        for r in range(pairs_ref.shape[1]):
            same = jnp.logical_and(
                pairs_ref[0:1, r : r + 1] - q_first == lane_block,
                pairs_ref[1:2, r : r + 1] == ga * p_blocks + p_block,
            )
            found = found + same.astype(jnp.int32)
        return found > 0

    live = [live_lanes(b) for b in range(p_blocks)]
    row_ids = lax.broadcasted_iota(jnp.int32, (BLK, rows), 0)

    def positive_mask(b):
        return row_ids == pos_ref[...] - (ga * p_blocks + b) * BLK

    tops, totals, hits = [], [], []
    for b in range(p_blocks):
        tile = scores[b * BLK : (b + 1) * BLK, :] * scale
        scores[b * BLK : (b + 1) * BLK, :] = tile
        top = jnp.max(tile, axis=0, keepdims=True)
        total = jnp.sum(jnp.exp(tile - top), axis=0, keepdims=True)
        tops.append(jnp.where(live[b], top, low_value))
        totals.append(jnp.where(live[b], total, 0.0))
        hits.append(jnp.sum(jnp.where(positive_mask(b), tile, 0.0), axis=0, keepdims=True))

    def merge(tops, totals):
        joint = functools.reduce(jnp.maximum, tops)
        return joint, sum(t * jnp.exp(m - joint) for m, t in zip(tops, totals))

    top, total = merge(tops, totals)
    stats[ga, 0:1, :] = top
    stats[ga, 1:2, :] = total
    stats[ga, 2:3, :] = sum(hits)
    stats[ga, 3:8, :] = jnp.zeros((5, rows), F32)

    def stat_copy(i):
        return remote(
            stats.at[ga],
            stats.at[ga],
            stat_send.at[i - 1],
            stat_recv.at[ga],
            pa=lax.rem(ga + i, n_pa),
        )

    for i in range(1, n_pa):
        stat_copy(i).start()
    for i in range(1, n_pa):
        other = lax.rem(ga + i, n_pa)
        arrived(stats.at[other], stat_recv.at[other])
    joint, total = merge(
        [stats[g, 0:1, :] for g in range(n_pa)], [stats[g, 1:2, :] for g in range(n_pa)]
    )
    log_norm = joint + jnp.log(total)
    losses_ref[...] = log_norm - sum(stats[g, 2:3, :] for g in range(n_pa))

    for b in range(p_blocks):
        tile = scores[b * BLK : (b + 1) * BLK, :]
        soft = jnp.where(live[b], jnp.exp(tile - log_norm), 0.0)
        weight = soft - positive_mask(b).astype(F32)
        scores[b * BLK : (b + 1) * BLK, :] = weight
        high, low = split(weight)
        split_w[0, b * BLK : (b + 1) * BLK, :] = high
        split_w[1, b * BLK : (b + 1) * BLK, :] = low

    def w_copy(i):
        target = lax.rem(x + i, nx) * 2 + core if i else sibling
        return remote(scores, weights_in.at[ga], w_send.at[i], w_recv.at[ga], pa=target)

    def w_forward(i):
        g = lax.rem(x + i, nx) * 2 + core
        return remote(weights_in.at[g], weights_in.at[g], w_pass.at[i], w_recv.at[g], pa=sibling)

    for i in range(nx):
        w_copy(i).start()
    if near:
        relay(relay_first)

    def form_partial(k):
        left = (split_w[0], split_w[1])
        for n in range(0, chunk, TILE):
            part = pl.ds(n, TILE)
            partial[k, :, part] = scale * dot3(
                left, (qhi[k, :, part], qlo[k, :, part]), ((1,), (0,))
            )

    def y_slot(zz, yy, e, h):
        return y_up.at[zz, yy - 1, halves[h]] if e > 0 else y_down.at[zz, yy, halves[h]]

    def y_sem(zz, yy, e, h):
        return y_recv.at[0 if e > 0 else 1, zz, yy - 1 if e > 0 else yy, h]

    def add_partial(k, h, slot, sem):
        arrived(slot, sem)
        partial[k, halves[h]] += slot[...]

    def y_sum(zz, yy, e, h):
        add_partial(zz * ny + yy, h, y_slot(zz, yy, e, h), y_sem(zz, yy, e, h))

    def y_partial(zz, yy, e, h):
        way = 0 if e > 0 else 1
        k = zz * ny + yy
        return remote(
            partial.at[k, halves[h]],
            y_slot(zz, yy, e, h),
            yr_send.at[way, k, h],
            y_sem(zz, yy, e, h),
            pb=z * ny + y + e,
        )

    def near_partial(d):
        way = 0 if d > 0 else 1
        return remote(
            partial.at[(z + d) * ny + 1 - y, halves[1]],
            near_in.at[way],
            near_out.at[way],
            near_recv.at[way],
            pb=(z + d) * ny + y,
        )

    def each_z(body, last):
        @pl.loop(0, nz - last)
        def _(i):
            s = nz - 1 - i
            for d in (1, -1):
                zz = z + d * s
                valid = inside(zz, nz) if d > 0 else jnp.logical_and(inside(zz, nz), s > 0)

                @pl.when(valid)
                def _(zz=zz, d=d):
                    body(zz, d, s)

    across = 1 - y
    farthest = jnp.maximum(z, nz - 1 - z)

    def across_each(s, act):
        for d in (1, -1) if not (isinstance(s, int) and s == 0) else (1,):
            for e in (1, -1):
                zz = z + d * s

                @pl.when(jnp.logical_and(inside(zz, nz), inside(y + e, ny)))
                def _(zz=zz, e=e):
                    act(zz, e)

    def across_start(s, h):
        across_each(s, lambda zz, e: y_partial(zz, across, e, h).start())

    def across_sent(s, h):
        across_each(s, lambda zz, e: y_partial(zz, across, e, h).wait_send())

    if near:
        def form_across(zz, d, s):
            form_partial(zz * ny + across)
            when_start(s == 1, lambda: near_partial(d))

            @pl.when(s == farthest)
            def _():
                for e in (1, -1):
                    when_start(inside(y + e, ny), lambda e=e: y_partial(zz, across, e, 0))

        each_z(form_across, 0)
        across_start(farthest, 1)
    else:
        for t in range(ny - 1, 0, -1):
            for e in (1, -1):
                yy = y + e * t

                @pl.when(inside(yy, ny))
                def _(yy=yy, e=e):
                    def send_one(zz, d, s):
                        form_partial(zz * ny + yy)
                        for h in range(2):

                            @pl.when(inside(y - e, ny))
                            def _(h=h):
                                y_sum(zz, yy, e, h)

                            y_partial(zz, yy, e, h).start()

                    each_z(send_one, 0)

    each_z(lambda zz, d, s: form_partial(zz * ny + y), 0)

    def across_next(s, h):
        if s > 1 or h == 0:

            @pl.when(farthest >= s)
            def _():
                across_sent(s, h)
                if s > 2 or h == 0:
                    across_start(s - 1, h)

        if s == 1 and h == 1:
            for d in (1, -1):
                way = 0 if d > 0 else 1

                @pl.when(inside(z - d, nz))
                def _(way=way):
                    add_partial(z * ny + across, 1, near_in.at[way], near_recv.at[way])

            across_start(0, 1)

    def z_slot(zz, d, h):
        return z_up.at[zz - 1, halves[h]] if d > 0 else z_down.at[zz, halves[h]]

    def z_sem(zz, d, h):
        return z_recv.at[0 if d > 0 else 1, zz - 1 if d > 0 else zz, h]

    def z_partial(zz, d, h):
        way = 0 if d > 0 else 1
        return remote(
            partial.at[zz * ny + y, halves[h]],
            z_slot(zz, d, h),
            zr_send.at[way, zz, h],
            z_sem(zz, d, h),
            pb=(z + d) * ny + y,
        )

    def y_gather(zz, h):
        for e in (1, -1):

            @pl.when(inside(y - e, ny))
            def _(e=e):
                y_sum(zz, y, e, h)

    def z_sum(zz, d, h):
        add_partial(zz * ny + y, h, z_slot(zz, d, h), z_sem(zz, d, h))

    def z_step(s):
        for h in range(2):
            if near:
                across_next(s, h)
            for d in (1, -1):
                zz = z + d * s

                @pl.when(inside(zz, nz))
                def _(zz=zz, d=d, h=h):
                    if not (near and s == 1 and h == 1):
                        y_gather(zz, h)

                    @pl.when(inside(z - d, nz))
                    def _():
                        z_sum(zz, d, h)

                    z_partial(zz, d, h).start()

    def add_query_grad(w_ref, p_refs, first):
        for j in range(ratio):
            high, low = split(p_refs[j][...])
            split_p[j, 0] = high
            split_p[j, 1] = low

        @pl.loop(0, rows // TILE)
        def _(t):
            part = pl.ds(pl.multiple_of(t * TILE, TILE), TILE)
            left = split(w_ref[:, part].T)
            for j in range(ratio):
                cols = pl.ds(j * chunk, chunk)
                term = scale * dot3(left, (split_p[j, 0], split_p[j, 1]), ((1,), (0,)))
                if first:
                    qgrad[part, cols] = term
                else:
                    qgrad[part, cols] += term

    def group_query_grad(g):
        arrived(weights_in.at[g], w_recv.at[g])
        wait_slab(g)
        add_query_grad(weights_in.at[g], [slab.at[g, j] for j in range(ratio)], False)

    def wait_slab(g):
        for j in range(ratio):
            for h in range(2):
                waited = False
                if near and h == 1:
                    waited = jnp.logical_and(jnp.logical_and(relays, g // 2 != x), y == j)

                @pl.when(jnp.logical_not(waited))
                def _(j=j, h=h):
                    arrived(slab.at[g, j, halves[h]], slab_recv.at[g, j, h])

    def same_core_query_grad(i):
        g = lax.rem(x + i, nx) * 2 + core
        wait_slab(g)
        add_query_grad(weights_in.at[g], [slab.at[g, j] for j in range(ratio)], False)

    z_step(nz - 1)
    add_query_grad(scores, [feats.at[ga * ratio + j] for j in range(ratio)], True)
    @pl.loop(0, n_pb)
    def _(k):
        held = jnp.logical_and(k // ny != z, k % ny != y)
        held = jnp.logical_and(held, k // ratio // 2 != x)
        when_start(jnp.logical_and(held, slab_needed(k, 1)), lambda: slab_feature(k, 1))

    group_query_grad(sibling)
    for s in range(nz - 2, 0, -1):
        z_step(s)
        if near and s == nz - 2:
            relay(relay_next)
    for i in range(1, nx):
        g = lax.rem(x + i, nx) * 2 + core
        arrived(weights_in.at[g], w_recv.at[g])
        w_forward(i).start()
    for i in range(1, nx):
        same_core_query_grad(i)
    for i in range(1, nx - 1):
        group_query_grad(lax.rem(x + i, nx) * 2 + 1 - core)
    out_copy = pltpu.make_async_copy(qgrad, qgrad_hbm, out_sem.at[0])
    out_copy.start()

    last = lax.rem(x + nx - 1, nx) * 2 + 1 - core
    arrived(weights_in.at[last], w_recv.at[last])
    w_out_copy = pltpu.make_async_copy(weights_in.at[last], w_out, out_sem.at[1])
    w_out_copy.start()
    wait_slab(last)
    slab_out_copy = pltpu.make_async_copy(slab.at[last], slab_out, out_sem.at[2])
    slab_out_copy.start()

    for h in range(2):
        for d in (1, -1):

            @pl.when(inside(z - d, nz))
            def _(d=d, h=h):
                z_sum(z, d, h)

        y_gather(z, h)

    pgrad_ref[...] = partial[me]

    @pl.loop(0, n_pb)
    def _(k):
        zz = k // ny
        yy = k % ny
        for h in range(2):
            when_sent(slab_needed(k, h), lambda: slab_feature(k, h))
        for h in range(2):
            far = jnp.abs(zz - z) != 1 if near and h == 1 else True
            unsent = zz == z if near else True
            for d in (1, -1):
                behind = zz <= z if d > 0 else zz >= z
                ahead = zz > z if d > 0 else zz < z
                line = yy == y
                when_sent(
                    jnp.logical_and(jnp.logical_and(line, behind), inside(z + d, nz)),
                    lambda d=d: z_feature(k, h, d),
                )
                when_sent(jnp.logical_and(line, ahead), lambda d=d: z_partial(zz, d, h))
            for e in (1, -1):
                behind = yy <= y if e > 0 else yy >= y
                ahead = yy > y if e > 0 else yy < y
                when_sent(
                    jnp.logical_and(far, jnp.logical_and(behind, inside(y + e, ny))),
                    lambda e=e: y_feature(k, h, e),
                )
                when_sent(jnp.logical_and(unsent, ahead), lambda e=e: y_partial(zz, yy, e, h))

    if near:
        for i in range(2):
            when_sent(relays, lambda i=i: relay_copy(i))
        for d in (1, -1):
            when_sent(inside(z + d, nz), lambda d=d: near_feature(d))
            when_sent(inside(z + d, nz), lambda d=d: near_partial(d))
    for i in range(1, n_pa):
        stat_copy(i).wait_send()
    for i in range(nx):
        w_copy(i).wait_send()
    for i in range(1, nx):
        w_forward(i).wait_send()
    out_copy.wait()
    w_out_copy.wait()
    slab_out_copy.wait()


def last_kernel(scale, so_far, weights, slab, out, split_p):
    ratio, _, chunk = slab.shape

    @pl.when(pl.program_id(0) == 0)
    def _():
        for j in range(ratio):
            high, low = split(slab[j])
            split_p[j, 0] = high
            split_p[j, 1] = low

    left = split(weights[...].T)
    for j in range(ratio):
        cols = pl.ds(j * chunk, chunk)
        term = dot3(left, (split_p[j, 0], split_p[j, 1]), ((1,), (0,)))
        out[:, cols] = so_far[:, cols] + scale * term


def body(n_pb, n_pa, queries, passages, pairs, positives):
    rows, width = queries.shape
    group_rows, chunk = passages.shape
    nx = n_pa // 2
    ny = nx
    nz = n_pb // ny
    ratio = n_pb // n_pa
    dma = pltpu.SemaphoreType.DMA
    losses, most, passage_grad, weights, slab = pl.pallas_call(
        functools.partial(kernel, n_pb, n_pa, math.sqrt(width)),
        out_shape=(
            jax.ShapeDtypeStruct((1, rows), F32),
            jax.ShapeDtypeStruct((rows, ratio * chunk), F32),
            jax.ShapeDtypeStruct((group_rows, chunk), F32),
            jax.ShapeDtypeStruct((group_rows, rows), F32),
            jax.ShapeDtypeStruct((ratio, group_rows, chunk), F32),
        ),
        in_specs=[
            pl.BlockSpec(memory_space=pl.ANY),
            pl.BlockSpec(memory_space=pl.ANY),
            pl.BlockSpec(memory_space=pltpu.VMEM),
            pl.BlockSpec(memory_space=pltpu.VMEM),
        ],
        out_specs=(
            pl.BlockSpec(memory_space=pltpu.VMEM),
            pl.BlockSpec(memory_space=pl.ANY),
            pl.BlockSpec(memory_space=pltpu.VMEM),
            pl.BlockSpec(memory_space=pl.ANY),
            pl.BlockSpec(memory_space=pl.ANY),
        ),
        scratch_shapes=[
            pltpu.VMEM((2, rows, chunk), F32),
            pltpu.VMEM((n_pb, rows, chunk), BF16),
            pltpu.VMEM((n_pb, rows, chunk), BF16),
            pltpu.VMEM((n_pb, group_rows, chunk), F32),
            pltpu.VMEM((n_pa, ratio, group_rows, chunk), F32),
            pltpu.VMEM((group_rows, rows), F32),
            pltpu.VMEM((n_pa, group_rows, rows), F32),
            pltpu.VMEM((n_pa, 8, rows), F32),
            pltpu.VMEM((n_pb, group_rows, chunk), F32),
            pltpu.VMEM((nz, ny - 1, group_rows, chunk), F32),
            pltpu.VMEM((nz, ny - 1, group_rows, chunk), F32),
            pltpu.VMEM((2, group_rows // 2, chunk), F32),
            pltpu.VMEM((nz - 1, group_rows, chunk), F32),
            pltpu.VMEM((nz - 1, group_rows, chunk), F32),
            pltpu.VMEM((rows, ratio * chunk), F32),
            pltpu.VMEM((2, group_rows, rows), BF16),
            pltpu.VMEM((ratio, 2, group_rows, chunk), BF16),
            dma((2,)),
            dma,
            dma((3,)),
            dma((n_pb, 2)),
            dma((2, n_pb, 2)),
            dma((2, n_pb, 2)),
            dma((2,)),
            dma((n_pb, 2)),
            dma((n_pa, ratio, 2)),
            dma((2,)),
            dma((n_pa - 1,)),
            dma((n_pa,)),
            dma((nx,)),
            dma((nx,)),
            dma((n_pa,)),
            dma((2, n_pb, 2)),
            dma((2, nz, ny - 1, 2)),
            dma((2,)),
            dma((2,)),
            dma((2, nz, 2)),
            dma((2, nz - 1, 2)),
        ],
        compiler_params=pltpu.CompilerParams(
            collective_id=0, has_side_effects=True, vmem_limit_bytes=62 * 2**20
        ),
    )(queries, passages, pairs.T, positives.reshape(1, rows))
    tile_spec = pl.BlockSpec((TILE, ratio * chunk), lambda t: (t, 0))
    query_grad = pl.pallas_call(
        functools.partial(last_kernel, math.sqrt(width)),
        grid=(rows // TILE,),
        out_shape=jax.ShapeDtypeStruct((rows, ratio * chunk), F32),
        in_specs=[
            tile_spec,
            pl.BlockSpec((group_rows, TILE), lambda t: (0, t)),
            pl.BlockSpec((ratio, group_rows, chunk), lambda t: (0, 0, 0)),
        ],
        out_specs=tile_spec,
        scratch_shapes=[pltpu.VMEM((ratio, 2, group_rows, chunk), BF16)],
        compiler_params=pltpu.CompilerParams(vmem_limit_bytes=62 * 2**20),
    )(most, weights, slab)
    return losses.reshape(-1), query_grad, passage_grad


def solution(mesh):
    in_specs = (P("pb", None), P("pa", "pb"), P("pb", None), P("pb"))
    out_specs = (P("pb"), P("pb", "pa"), P("pa", "pb"))
    return jax.shard_map(
        functools.partial(body, mesh.shape["pb"], mesh.shape["pa"]),
        mesh=mesh,
        in_specs=in_specs,
        out_specs=out_specs,
        check_vma=False,
    )
```
